32 devices in a mesh: seq: 4 (over x, core), shard: 8 (over z, y).
Axes of the slice: x: 2, y: 2, z: 4, core: 2. Of those that a mesh axis runs over, the one named last changes fastest.
Arguments:
- inputs: bfloat16 [16, 1024, 1024], P('shard', 'seq'), may hold values from -6 to 6
- cotangent: bfloat16 [16, 1024, 1024], P('shard', 'seq'), may hold values from -6 to 6
- ffn1_in: bfloat16 [1024, 4096], P('shard'), may hold values from -0.1875 to 0.1875
- ffn1_out: bfloat16 [4096, 1024], P('shard'), may hold values from -0.09375 to 0.09375
- attn_in: bfloat16 [1024, 3072], P('shard'), may hold values from -0.1875 to 0.1875
- attn_out: bfloat16 [1024, 1024], P('shard'), may hold values from -1.5 to 1.5
- conv_in: bfloat16 [1024, 2048], P('shard'), may hold values from -0.1875 to 0.1875
- conv_out: bfloat16 [1024, 1024], P('shard'), may hold values from -0.1875 to 0.1875
- ffn2_in: bfloat16 [1024, 4096], P('shard'), may hold values from -0.1875 to 0.1875
- ffn2_out: bfloat16 [4096, 1024], P('shard'), may hold values from -0.09375 to 0.09375
- depthwise: bfloat16 [1024, 31], P('shard'), may hold values from -1 to 1
- rel_table: bfloat16 [73, 64], replicated, may hold values from -6 to 6
- norm_gain: bfloat16 [1024, 6], P('shard'), may hold values from 0.25 to 1.75
- shifts: bfloat16 [1024, 10], P('shard'), may hold values from -3 to 3
- hidden_bias: bfloat16 [4096, 2], P('shard'), may hold values from -3 to 3
- attn_bias: bfloat16 [1024], P('shard'), may hold values from -3 to 3
- clip_threshold: float32 [16], replicated, may hold values from 3 to 30
Outputs:
- output: bfloat16 [16, 1024, 1024], P('shard', 'seq')
- input_grad: float32 [16, 1024, 1024], P('shard', 'seq')
- grad_ffn1_in: float32 [1024, 4096], P('shard')
- grad_ffn1_out: float32 [4096, 1024], P('shard')
- grad_attn_in: float32 [1024, 3072], P('shard')
- grad_attn_out: float32 [1024, 1024], P('shard')
- grad_conv_in: float32 [1024, 2048], P('shard')
- grad_conv_out: float32 [1024, 1024], P('shard')
- grad_ffn2_in: float32 [1024, 4096], P('shard')
- grad_ffn2_out: float32 [4096, 1024], P('shard')
- grad_depthwise: float32 [1024, 31], P('shard')
- grad_rel_table: float32 [73, 64], replicated
- grad_norm_gain: float32 [1024, 6], P('shard')
- grad_shifts: float32 [1024, 10], P('shard')
- grad_hidden_bias: float32 [4096, 2], P('shard')
- grad_attn_bias: float32 [1024], P('shard')
- head_max: float32 [16], replicated
- qk_scale: float32 [16], replicated
The draws below stay inside these ranges and needn't reach their ends.
All inputs are finite; a program needn't handle non-finite values.
Results may differ from the reference program's by a relative error of at most 0.019.
Values may be sent and summed in bfloat16 or wider, within the bound.
No kernel may reach another device: no remote copies, remote signals or barrier semaphores. Data moves between devices by JAX's collectives and lax.ppermute only.
A program may use at most 256 MiB of HBM per device.

```python
import functools
import math
import jax
import jax.numpy as jnp
from jax import lax

D = 1024
H = 16
HD = 64
FF = 4096
KER = 31
LEFT = 64
RIGHT = 8
REL = 73
FRAMES = 1024
CLIPS = 16


def block_levels(own_key, dims, split, least, top_value):
    loudness, own = 1.0, jax.random.fold_in(own_key, 6)
    for dim, parts in split:
        steps = jnp.exp(jax.random.uniform(jax.random.fold_in(own, dim), (parts,), jnp.float32, least / len(split), top_value / len(split)))
        loudness = loudness * jnp.repeat(steps, dims[dim] // parts).reshape([-1 if axis == dim else 1 for axis in range(len(dims))])
    return loudness


def bell_draw(rng, shape, deviation, bound, split=(), kind=jnp.bfloat16):
    values = deviation * jax.random.normal(rng, shape, jnp.float32)
    if split:
        values = values * block_levels(rng, shape, split, -0.22, 0.18)
    return jnp.clip(values, -bound, bound).astype(kind)


def setup_inputs(seed: int = 0) -> dict:
    seeds = jax.random.split(jax.random.key(seed), 18)
    return {
        "inputs": bell_draw(seeds[0], (CLIPS, FRAMES, D), 1.0, 6.0, ((0, 8), (1, 4))),
        "cotangent": bell_draw(seeds[1], (CLIPS, FRAMES, D), 1.0, 6.0, ((0, 8), (1, 4))),
        "ffn1_in": bell_draw(seeds[2], (D, FF), D ** -0.5, 0.1875, ((0, 8),)),
        "ffn1_out": bell_draw(seeds[3], (FF, D), FF ** -0.5, 0.09375, ((0, 8),)),
        "attn_in": bell_draw(seeds[4], (D, 3 * D), D ** -0.5, 0.1875, ((0, 8),)),
        "attn_out": bell_draw(seeds[5], (D, D), (D // 64) ** -0.5, 1.5, ((0, 8),)),
        "conv_in": bell_draw(seeds[6], (D, 2 * D), D ** -0.5, 0.1875, ((0, 8),)),
        "conv_out": bell_draw(seeds[7], (D, D), D ** -0.5, 0.1875, ((0, 8),)),
        "ffn2_in": bell_draw(seeds[8], (D, FF), D ** -0.5, 0.1875, ((0, 8),)),
        "ffn2_out": bell_draw(seeds[9], (FF, D), FF ** -0.5, 0.09375, ((0, 8),)),
        "depthwise": bell_draw(seeds[10], (D, KER), KER ** -0.5, 1.0, ((0, 8),)),
        "rel_table": bell_draw(seeds[11], (REL, HD), 1.0, 6.0),
        "norm_gain": jnp.clip(1.0 + 0.15 * jax.random.normal(seeds[12], (D, 6), jnp.float32), 0.25, 1.75).astype(jnp.bfloat16),
        "shifts": bell_draw(seeds[13], (D, 10), 0.5, 3.0, ((0, 8),)),
        "hidden_bias": bell_draw(seeds[14], (FF, 2), 0.5, 3.0, ((0, 8),)),
        "attn_bias": bell_draw(seeds[15], (D,), 0.5, 3.0, ((0, 8),)),
        "clip_threshold": jnp.clip(jnp.exp(jax.random.uniform(seeds[16], (H,), jnp.float32, math.log(3.0), math.log(30.0))), 3.0, 30.0),
    }


@jax.custom_vjp
def low(v):
    return lax.optimization_barrier(v.astype(jnp.bfloat16)).astype(jnp.float32)

@jax.custom_vjp
def low_back(v):
    return v

def low_keep(v):
    return (low(v), None)

def low_pass(kept, grad):
    return (grad,)

def back_keep(v):
    return (v, None)

def back_low(kept, grad):
    return (low(grad),)
low.defvjp(low_keep, low_pass)
low_back.defvjp(back_keep, back_low)
EPS = 1e-05
HIGH = lax.Precision.HIGHEST

def matmul_high(left_op, right_op):
    return jnp.matmul(left_op, right_op, precision=HIGH)

def layer_norm(stream, gain_vec, shift_vec):
    average = lax.optimization_barrier(jnp.mean(stream, axis=-1, keepdims=True))
    centred = stream - average
    variance = lax.optimization_barrier(jnp.mean(centred * centred, axis=-1, keepdims=True))
    return centred * lax.rsqrt(variance + EPS) * gain_vec + shift_vec

def silu_act(stream):
    return stream * jax.nn.sigmoid(stream)

def clip_attention(pieces, rel_rows):
    queries, keys_all, values_all = pieces
    length = queries.shape[1]
    places = jnp.arange(length, dtype=jnp.int32)
    distance = (jnp.clip(places[None, :] - places[:, None], -LEFT, RIGHT) + LEFT).astype(jnp.int32)

    def one_head(query_head, key_head, value_head):
        related = matmul_high(query_head, rel_rows.T)
        scores = matmul_high(query_head, key_head.T) + jnp.take_along_axis(related, distance, axis=1)
        scores = low_back(scores * HD ** (-0.5))
        head_peak = jnp.max(scores)
        shifted = scores - lax.optimization_barrier(jnp.max(scores, axis=1, keepdims=True))
        exponents = jnp.exp(shifted)
        softmax_w = exponents / lax.optimization_barrier(jnp.sum(exponents, axis=1, keepdims=True))
        return (matmul_high(low(softmax_w), value_head), head_peak)
    return jax.vmap(one_head)(queries, keys_all, values_all)

def feed_forward(stream, column, gains, shifts, weight_in, bias_in, weight_out, bias_out):
    normed = low(layer_norm(stream, gains[:, column], shifts[:, column]))
    hidden = low_back(matmul_high(normed, weight_in) + bias_in)
    return low_back(matmul_high(low(silu_act(hidden)), weight_out) + bias_out)

def forward(clip_block, weights):
    ffn1_in, ffn1_out, attn_in, attn_out, conv_in, conv_out, ffn2_in, ffn2_out, depthwise, rel_table, norm_gain, shifts, hidden_bias, attn_bias = weights
    clip_count, length, feature_width = clip_block.shape
    stream = clip_block.reshape(clip_count * length, feature_width)
    stream = stream + 0.5 * feed_forward(stream, 0, norm_gain, shifts, ffn1_in, hidden_bias[:, 0], ffn1_out, shifts[:, 6])
    normed = low(layer_norm(stream, norm_gain[:, 1], shifts[:, 1]))
    projected = matmul_high(normed, attn_in)
    queries = low(low_back(projected[:, :feature_width] + shifts[:, 8]))
    keys_all = low(low_back(projected[:, feature_width:2 * feature_width]))
    values_all = low(low_back(projected[:, 2 * feature_width:] + shifts[:, 9]))

    def head_major(matrix):
        return matrix.reshape(clip_count, length, H, HD).transpose(0, 2, 1, 3)
    attend = jax.checkpoint(functools.partial(clip_attention, rel_rows=rel_table))
    attended, head_peaks = lax.map(attend, (head_major(queries), head_major(keys_all), head_major(values_all)))
    attended = attended.transpose(0, 2, 1, 3).reshape(clip_count * length, feature_width)
    attended = low(low_back(attended))
    stream = stream + low_back(matmul_high(attended, attn_out) + attn_bias)
    normed = low(layer_norm(stream, norm_gain[:, 2], shifts[:, 2]))
    mixing = low_back(matmul_high(normed, conv_in))
    gated_half = low(mixing[:, :feature_width] * jax.nn.sigmoid(mixing[:, feature_width:]))
    gated_half = gated_half.reshape(clip_count, length, feature_width)
    padded = jnp.pad(gated_half, ((0, 0), (KER - 1, 0), (0, 0)))
    convolved = jnp.zeros_like(gated_half)
    for tap_index in range(KER):
        convolved = convolved + padded[:, tap_index:tap_index + length, :] * depthwise[:, tap_index]
    convolved = low_back(convolved.reshape(clip_count * length, feature_width))
    activated = low(silu_act(layer_norm(convolved, norm_gain[:, 3], shifts[:, 3])))
    stream = stream + low_back(matmul_high(activated, conv_out))
    stream = stream + 0.5 * feed_forward(stream, 4, norm_gain, shifts, ffn2_in, hidden_bias[:, 1], ffn2_out, shifts[:, 7])
    result = layer_norm(stream, norm_gain[:, 5], shifts[:, 5])
    return (result.reshape(clip_count, length, feature_width), lax.optimization_barrier(jnp.max(head_peaks, axis=0)))

def reference(inputs, cotangent, ffn1_in, ffn1_out, attn_in, attn_out, conv_in, conv_out, ffn2_in, ffn2_out, depthwise, rel_table, norm_gain, shifts, hidden_bias, attn_bias, clip_threshold):
    weights = tuple((entry.astype(jnp.float32) for entry in (ffn1_in, ffn1_out, attn_in, attn_out, conv_in, conv_out, ffn2_in, ffn2_out, depthwise, rel_table, norm_gain, shifts, hidden_bias, attn_bias)))
    clip_count, length, feature_width = inputs.shape
    group_size = math.gcd(clip_count, max(1, 4096 // length))
    group_count = clip_count // group_size
    blocks_in = inputs.astype(jnp.float32).reshape(group_count, group_size, length, feature_width)
    blocks_cot = cotangent.astype(jnp.float32).reshape(group_count, group_size, length, feature_width)

    def group_step(running, pieces):
        totals, peak_so_far = running
        block_in, block_cot = pieces
        result, pullback, head_peaks = jax.vjp(forward, block_in, weights, has_aux=True)
        grad_in, grad_weights = pullback(block_cot)
        totals = jax.tree.map(jnp.add, totals, grad_weights)
        return ((totals, jnp.maximum(peak_so_far, head_peaks)), (result.astype(jnp.bfloat16), grad_in))
    initial = (jax.tree.map(jnp.zeros_like, weights), jnp.full((H,), -1e+30, dtype=jnp.float32))
    (totals, head_max), (outputs, grads_in) = lax.scan(group_step, initial, (blocks_in, blocks_cot))
    qk_scale = jnp.sqrt(clip_threshold / jnp.maximum(head_max, clip_threshold))
    output = outputs.reshape(clip_count, length, feature_width)
    input_grad = grads_in.reshape(clip_count, length, feature_width)
    return (output, input_grad, totals[0], totals[1], totals[2], totals[3], totals[4], totals[5], totals[6], totals[7], totals[8], totals[9], totals[10], totals[11], totals[12], totals[13], head_max, qk_scale)
```

```python
import functools

import jax
import jax.numpy as jnp
from jax import lax
from jax.experimental import pallas as pl
from jax.experimental.pallas import tpu as pltpu
from jax.sharding import Mesh, PartitionSpec as P

H = 16
HD = 64
KER = 31
LEFT = 64
RIGHT = 8
REL = 73
SUB = 128
BAND = 512


EPS = 1e-05
HIGH = lax.Precision.HIGHEST


def from_behind(value, axis, steps):
    count = lax.axis_size(axis)
    leading, last = (max(0, -steps), min(count, count - steps))
    return lax.ppermute(value, axis, [(source, source + steps) for source in range(leading, last)])


def matmul(left_op, right_op):
    return jnp.dot(left_op, right_op, preferred_element_type=jnp.float32)


def outer_rows(left_op, right_op):
    return lax.dot_general(
        left_op, right_op, (((0,), (0,)), ((), ())), preferred_element_type=jnp.float32
    )


def inner_cols(left_op, right_op):
    return lax.dot_general(
        left_op, right_op, (((1,), (1,)), ((), ())), preferred_element_type=jnp.float32
    )


def layer_norm(stream, gain_vec, shift_vec):
    average = jnp.mean(stream, axis=-1, keepdims=True)
    centred = stream - average
    variance = jnp.mean(centred * centred, axis=-1, keepdims=True)
    return centred * lax.rsqrt(variance + EPS) * gain_vec + shift_vec


def silu_act(stream):
    return stream * jax.nn.sigmoid(stream)


def norm_silu(stream, gain_vec, shift_vec):
    return silu_act(layer_norm(stream, gain_vec, shift_vec))


def gate_linear(mixing):
    half_width = mixing.shape[1] // 2
    return mixing[:, :half_width] * jax.nn.sigmoid(mixing[:, half_width:])


def dot_tt(left_op, right_op):
    return lax.dot_general(left_op, right_op, (((1,), (1,)), ((), ())), preferred_element_type=jnp.float32)


def dot_nn(left_op, right_op):
    return lax.dot_general(left_op, right_op, (((1,), (0,)), ((), ())), preferred_element_type=jnp.float32)


def dot_tn(left_op, right_op):
    return lax.dot_general(left_op, right_op, (((0,), (0,)), ((), ())), preferred_element_type=jnp.float32)


def relative_rows(rel_table):
    distance = jnp.clip(jnp.arange(BAND, dtype=jnp.int32) - BAND // 2, -LEFT, RIGHT) + LEFT
    rows = jnp.take(rel_table, distance, axis=0)
    return jnp.concatenate([rows, rows], axis=1)


def side_columns(order, me, frames):
    groups = frames // SUB
    chunk = jnp.repeat(order, frames)
    block = chunk * groups + jnp.tile(jnp.arange(frames, dtype=jnp.int32) // SUB, order.shape[0])
    columns = []
    for group in range(groups):
        place = me * groups + group
        columns += [block < place - 1, block > place + 1]
    marks = jnp.stack(columns, axis=1).astype(jnp.bfloat16)
    return jnp.pad(marks, ((0, 0), (0, 128 - marks.shape[1])))


def place_bias(scores, base, where, me, frames, chunks):
    groups = frames // SUB
    left, right = base[:, :1], base[:, BAND - 1 :]
    for group in range(groups):
        rows = slice(group * SUB, (group + 1) * SUB)
        own = me * groups + group
        for chunk in range(chunks):
            for part in range(groups):
                block = where[chunk] * groups + part
                col = (chunk * groups + part) * SUB
                side = jnp.where(block <= own, left[rows], right[rows])
                scores[rows, col : col + SUB] = scores[rows, col : col + SUB] + side
        band = pltpu.roll(base[rows], BAND - SUB, 1, stride=1, stride_axis=0)
        for step in (-1, 0, 1):
            chunk_step = (group + step) // groups
            part = (group + step) % groups
            place = where[chunks + 1 + chunk_step]

            @pl.when(place >= 0)
            def _():
                col = pl.multiple_of((place * groups + part) * SUB, SUB)
                side = right[rows] if step > 0 else left[rows]
                piece = band[:, (step + 1) * SUB : (step + 2) * SUB]
                scores[rows, pl.ds(col, SUB)] = scores[rows, pl.ds(col, SUB)] + (piece - side)


def attend_kernel(frames, chunks, where, q_ref, k_ref, v_ref, rel_ref, o_ref, top_ref, log_ref, scores):
    pair = pl.program_id(1)
    me = where[2 * chunks - chunks + 3]
    query = q_ref[...]
    keys = k_ref[...].reshape(chunks * frames, 2 * HD)
    values = v_ref[...].reshape(chunks * frames, 2 * HD)
    lane = lax.broadcasted_iota(jnp.int32, (frames, 2 * HD), 1)
    outs = []
    for half in range(2):
        inside = (lane // HD) == half
        query_half = jnp.where(inside, query, 0) * jnp.bfloat16(HD ** (-0.5))
        scores[...] = dot_tt(query_half, keys)
        base = dot_tt(query_half, rel_ref[...])
        place_bias(scores, base, where, me, frames, chunks)
        full = scores[...]
        top = jnp.max(full, axis=1, keepdims=True)
        weights = jnp.exp(full - top)
        total = jnp.sum(weights, axis=1, keepdims=True)
        outs.append(dot_nn(weights.astype(jnp.bfloat16), values) * (1.0 / total))
        here = lane == pair * 2 + half
        top_ref[...] = jnp.where(here, top, top_ref[...])
        log_ref[...] = jnp.where(here, top + jnp.log(total), log_ref[...])
    o_ref[...] = jnp.where(lane < HD, outs[0], outs[1]).astype(o_ref.dtype)


def attend_back_kernel(
    frames, chunks, where, q_ref, k_ref, v_ref, do_ref, o_ref, log_ref, rel_ref, side_ref, ends_ref, flip_ref,
    dq_ref, dk_ref, dv_ref, gt_ref, ge_ref, scores, window
):
    clip, pair = pl.program_id(0), pl.program_id(1)
    me = where[2 * chunks - chunks + 3]
    groups = frames // SUB
    query, grad = q_ref[...], do_ref[...]
    keys = k_ref[...].reshape(chunks * frames, 2 * HD)
    values = v_ref[...].reshape(chunks * frames, 2 * HD)
    keys_side = jnp.concatenate([keys, side_ref[...]], axis=1)
    lane = lax.broadcasted_iota(jnp.int32, (frames, 2 * HD), 1)
    product = grad.astype(jnp.float32) * o_ref[...].astype(jnp.float32)

    @pl.when((clip == 0) & (pair == 0))
    def _():
        gt_ref[...] = jnp.zeros_like(gt_ref)
        ge_ref[...] = jnp.zeros_like(ge_ref)

    parts = []
    for half in range(2):
        inside = (lane // HD) == half
        query_half = jnp.where(inside, query, 0) * jnp.bfloat16(HD ** (-0.5))
        grad_half = jnp.where(inside, grad, 0)
        scores[...] = dot_tt(query_half, keys)
        base = dot_tt(query_half, rel_ref[...])
        place_bias(scores, base, where, me, frames, chunks)
        log_total = jnp.sum(jnp.where(lane == pair * 2 + half, log_ref[...], 0.0), axis=1, keepdims=True)
        delta = jnp.sum(jnp.where(inside, product, 0.0), axis=1, keepdims=True)
        weights = jnp.exp(scores[...] - log_total)
        grad_weights = dot_tt(grad_half, values)
        grad_scores = (weights * (grad_weights - delta)).astype(jnp.bfloat16)
        window[...] = grad_scores
        grad_values = dot_tn(weights.astype(jnp.bfloat16), grad)
        grad_keys = dot_tn(grad_scores, query) * HD ** (-0.5)
        wide = dot_nn(grad_scores, keys_side)
        grad_query = wide[:, : 2 * HD]
        pieces = []
        for group in range(groups):
            rows = slice(group * SUB, (group + 1) * SUB)
            bands = []
            for step in (-1, 0, 1):
                chunk_step = (group + step) // groups
                part = (group + step) % groups
                place = where[chunks + 1 + chunk_step]
                col = pl.multiple_of((jnp.maximum(place, 0) * groups + part) * SUB, SUB)
                held = window[rows, pl.ds(col, SUB)]
                bands.append(jnp.where(place >= 0, held, jnp.zeros_like(held)))
            flipped = dot_nn(flip_ref[...], jnp.concatenate(bands, axis=1))
            flipped = jnp.concatenate([flipped, jnp.zeros((SUB, SUB), jnp.float32)], axis=1)
            turned = pltpu.roll(flipped, 1, 1, stride=1, stride_axis=0).astype(jnp.bfloat16)
            turned = dot_nn(flip_ref[...], turned).astype(jnp.bfloat16)
            left = wide[rows, 2 * HD + 2 * group : 2 * HD + 2 * group + 1]
            right = wide[rows, 2 * HD + 2 * group + 1 : 2 * HD + 2 * group + 2]
            pieces.append(
                grad_query[rows] + dot_nn(turned, rel_ref[...]) + left * ends_ref[:1] + right * ends_ref[1:2]
            )
            gt_ref[...] += dot_tn(turned, query_half[rows])
            query_wide = query_half[rows].astype(jnp.float32)
            ge_ref[0:1] += jnp.sum(left * query_wide, axis=0, keepdims=True)
            ge_ref[1:2] += jnp.sum(right * query_wide, axis=0, keepdims=True)
        parts.append((jnp.concatenate(pieces, axis=0) * HD ** (-0.5), grad_keys, grad_values))
    dq_ref[...] = jnp.where(lane < HD, parts[0][0], parts[1][0]).astype(dq_ref.dtype)
    lane_keys = lax.broadcasted_iota(jnp.int32, (chunks * frames, 2 * HD), 1) < HD
    dk_ref[...] = jnp.where(lane_keys, parts[0][1], parts[1][1]).astype(dk_ref.dtype).reshape(dk_ref.shape)
    dv_ref[...] = jnp.where(lane_keys, parts[0][2], parts[1][2]).astype(dv_ref.dtype).reshape(dv_ref.shape)


def where_vector(order, me):
    places = []
    for step in (-1, 0, 1):
        match = order == me + step
        places.append(jnp.where(jnp.any(match), jnp.argmax(match), -1))
    return jnp.concatenate([order, jnp.stack(places), me[None]]).astype(jnp.int32)


def attend(query, keys_values, where, rel_wide):
    chunks, clips, frames, double = keys_values.shape
    width = double // 2
    pairs = width // (2 * HD)
    rows = lambda clip, pair, where: (clip, pair)
    stats = pl.BlockSpec((frames, 128), lambda clip, pair, where: (clip, 0))
    kv_block = (chunks, pl.Squeezed(), frames, 2 * HD)
    return pl.pallas_call(
        functools.partial(attend_kernel, frames, chunks),
        grid_spec=pltpu.PrefetchScalarGridSpec(
            num_scalar_prefetch=1,
            grid=(clips, pairs),
            in_specs=[
                pl.BlockSpec((frames, 2 * HD), rows),
                pl.BlockSpec(kv_block, lambda clip, pair, where: (0, clip, 0, pair)),
                pl.BlockSpec(kv_block, lambda clip, pair, where: (0, clip, 0, pairs + pair)),
                pl.BlockSpec((BAND, 2 * HD), lambda clip, pair, where: (0, 0)),
            ],
            out_specs=[pl.BlockSpec((frames, 2 * HD), rows), stats, stats],
            scratch_shapes=[pltpu.VMEM((frames, chunks * frames), jnp.float32)],
        ),
        out_shape=[
            jax.ShapeDtypeStruct((clips * frames, width), jnp.bfloat16),
            jax.ShapeDtypeStruct((clips * frames, 128), jnp.float32),
            jax.ShapeDtypeStruct((clips * frames, 128), jnp.float32),
        ],
        compiler_params=pltpu.CompilerParams(vmem_limit_bytes=48 * 2**20),
        name="attend",
    )(where, query, keys_values, keys_values, rel_wide)


def attend_back(query, keys_values, grad, attended, log_totals, where, rel_wide, sides):
    chunks, clips, frames, double = keys_values.shape
    width = double // 2
    pairs = width // (2 * HD)
    rows = pl.BlockSpec((frames, 2 * HD), lambda clip, pair, where: (clip, pair))
    stats = pl.BlockSpec((frames, 128), lambda clip, pair, where: (clip, 0))
    kv_block = (chunks, pl.Squeezed(), frames, 2 * HD)
    first = pl.BlockSpec(kv_block, lambda clip, pair, where: (0, clip, 0, pair))
    second = pl.BlockSpec(kv_block, lambda clip, pair, where: (0, clip, 0, pairs + pair))
    fixed = lambda shape: pl.BlockSpec(shape, lambda clip, pair, where: (0, 0))
    ends = jnp.concatenate([rel_wide[:1], rel_wide[-1:], jnp.zeros((6, 2 * HD), rel_wide.dtype)]).astype(jnp.float32)
    kv_shape = jax.ShapeDtypeStruct((chunks, clips, frames, width), jnp.bfloat16)
    return pl.pallas_call(
        functools.partial(attend_back_kernel, frames, chunks),
        grid_spec=pltpu.PrefetchScalarGridSpec(
            num_scalar_prefetch=1,
            grid=(clips, pairs),
            in_specs=[rows, first, second, rows, rows, stats, fixed((BAND, 2 * HD)), fixed((chunks * frames, 128)), fixed((8, 2 * HD)), fixed((SUB, SUB))],
            out_specs=[rows, first, first, fixed((BAND, 2 * HD)), fixed((8, 2 * HD))],
            scratch_shapes=[
                pltpu.VMEM((frames, chunks * frames), jnp.float32),
                pltpu.VMEM((frames, chunks * frames), jnp.bfloat16),
            ],
        ),
        out_shape=[
            jax.ShapeDtypeStruct(query.shape, jnp.bfloat16),
            kv_shape,
            kv_shape,
            jax.ShapeDtypeStruct((BAND, 2 * HD), jnp.float32),
            jax.ShapeDtypeStruct((8, 2 * HD), jnp.float32),
        ],
        compiler_params=pltpu.CompilerParams(vmem_limit_bytes=48 * 2**20),
        name="attend_back",
    )(where, query, keys_values, keys_values, grad, attended, log_totals, rel_wide, sides, ends, jnp.eye(SUB, dtype=jnp.bfloat16)[::-1])


def table_grad(grad_band, grad_ends):
    distance = jnp.clip(jnp.arange(BAND, dtype=jnp.int32) - BAND // 2, -LEFT, RIGHT) + LEFT
    both = grad_band[:, :HD] + grad_band[:, HD:]
    ends = grad_ends[:2, :HD] + grad_ends[:2, HD:]
    first = BAND // 2 - LEFT
    middle = both[first : first + REL]
    low = jnp.sum(both[:first], axis=0) + ends[0]
    high = jnp.sum(both[first + REL :], axis=0) + ends[1]
    return jnp.concatenate([middle[:1] + low, middle[1:-1], middle[-1:] + high])


def feed_forward(stream, gain_vec, shift_vec, weight_in, bias_in, weight_out, bias_out):
    normed, pull_norm = jax.vjp(layer_norm, stream, gain_vec, shift_vec)
    normed = normed.astype(jnp.bfloat16)
    hidden = matmul(normed, weight_in) + bias_in
    active, pull_act = jax.vjp(silu_act, hidden)
    active = active.astype(jnp.bfloat16)
    branch = matmul(active, weight_out) + bias_out
    return (stream + 0.5 * branch, (normed, pull_norm, active, pull_act))


def feed_back(grad_stream, kept, weight_in, weight_out):
    normed, pull_norm, active, pull_act = kept
    grad_branch = (0.5 * grad_stream).astype(jnp.bfloat16)
    grad_out_w = outer_rows(active, grad_branch)
    grad_out_b = jnp.sum(grad_branch.astype(jnp.float32), axis=0)
    grad_hidden = pull_act(inner_cols(grad_branch, weight_out))[0].astype(jnp.bfloat16)
    grad_in_w = outer_rows(normed, grad_hidden)
    grad_in_b = jnp.sum(grad_hidden.astype(jnp.float32), axis=0)
    grad_normed, grad_gain, grad_shift = pull_norm(inner_cols(grad_hidden, weight_in))
    return (
        grad_stream + grad_normed,
        (grad_in_w, grad_in_b, grad_out_w, grad_out_b, grad_gain, grad_shift),
    )


def refine(mesh):
    seq, shard = (mesh.shape["seq"], mesh.shape["shard"])
    devices = mesh.devices.reshape(seq // 2, 2, shard // 2, 2)
    return Mesh(devices, ("x", "core", "z", "y"))


SEQ = ("x", "core")
SHARD = ("z", "y")
SWAP = [(0, 1), (1, 0)]


def own_columns(weight):
    parts = lax.axis_size("x") * 2
    width = weight.shape[1] // parts
    place = lax.axis_index("core") * lax.axis_size("x") + lax.axis_index("x")
    return lax.dynamic_slice_in_dim(weight, place * width, width, axis=1)


def join(value, axis_name, axis):
    if lax.axis_size(axis_name) != 2:
        return lax.all_gather(value, axis_name, axis=axis)
    other = lax.ppermute(value, axis_name, SWAP)
    first = lax.axis_index(axis_name) == 0
    return jnp.stack([jnp.where(first, value, other), jnp.where(first, other, value)], axis=axis)


def collect_chunks(value):
    me = lax.axis_index(SEQ)
    if lax.axis_size("x") != 2:
        return lax.all_gather(value, SEQ, axis=0), jnp.arange(lax.axis_size(SEQ), dtype=jnp.int32)
    beside = lax.ppermute(value, "core", SWAP)
    near = jnp.stack([value, beside])
    far = lax.ppermute(near, "x", SWAP)
    return jnp.concatenate([near, far]), jnp.bitwise_xor(me, jnp.arange(4, dtype=jnp.int32))


def return_chunks(value):
    if lax.axis_size("x") != 2:
        return lax.psum_scatter(value, SEQ, scatter_dimension=0, tiled=True)[0]
    got = lax.ppermute(value[1::2], "core", SWAP)
    value = (value[::2].astype(jnp.float32) + got.astype(jnp.float32)).astype(jnp.bfloat16)
    got = lax.ppermute(value[1], "x", SWAP)
    return (value[0].astype(jnp.float32) + got.astype(jnp.float32)).astype(jnp.bfloat16)


def gather_weights(parts, order):
    value = jnp.concatenate([own_columns(part) for part in parts], axis=1)
    rows, width = value.shape
    value = lax.all_gather(value, "z", axis=0)
    for axis_name in order:
        if axis_name == "y":
            value = join(value, "y", value.ndim - 2)
        else:
            value = join(value, "x", 0)
    value = lax.all_gather(value, "core", axis=0)
    return value.reshape(-1, rows * lax.axis_size("z") * 2, width)


def whole(blocks, start, width):
    part = blocks[:, :, start : start + width]
    return jnp.transpose(part, (1, 0, 2)).reshape(part.shape[1], -1)


def halve(value, axis_name, axis):
    if lax.axis_size(axis_name) != 2:
        return jnp.squeeze(
            lax.psum_scatter(value, axis_name, scatter_dimension=axis, tiled=True), axis
        )
    mine = lax.axis_index(axis_name)
    sent = lax.dynamic_index_in_dim(value, 1 - mine, axis, keepdims=False)
    kept = lax.dynamic_index_in_dim(value, mine, axis, keepdims=False)
    got = lax.ppermute(sent, axis_name, SWAP)
    return (kept.astype(jnp.float32) + got.astype(jnp.float32)).astype(jnp.bfloat16)


def scatter_grads(grads, order):
    holders = lax.axis_size("x") * 2
    depth = lax.axis_size("z")
    blocks = [
        jnp.transpose(
            grad.astype(jnp.bfloat16).reshape(grad.shape[0], holders, -1), (1, 0, 2)
        )
        for grad in grads
    ]
    value = jnp.concatenate(blocks, axis=2)
    rows, width = (value.shape[1], value.shape[2])
    value = value.reshape(2, holders // 2, depth, 2, rows // depth // 2, width)
    value = lax.psum_scatter(value, "core", scatter_dimension=0, tiled=True)[0]
    for axis_name in order:
        if axis_name == "y":
            value = halve(value, "y", value.ndim - 3)
        else:
            value = halve(value, "x", 0)
    value = lax.psum_scatter(value, "z", scatter_dimension=0, tiled=True)[0]
    value = lax.all_gather(value, ("core", "x"), axis=0)
    results = []
    start = 0
    for grad in grads:
        piece = grad.shape[1] // holders
        part = value[:, :, start : start + piece]
        results.append(
            jnp.transpose(part, (1, 0, 2)).reshape(part.shape[1], -1).astype(jnp.float32)
        )
        start = start + piece
    return results


def local(
    inputs,
    cotangent,
    ffn1_in,
    ffn1_out,
    attn_in,
    attn_out,
    conv_in,
    conv_out,
    ffn2_in,
    ffn2_out,
    depthwise,
    rel_table,
    norm_gain,
    shifts,
    hidden_bias,
    attn_bias,
    clip_threshold,
):
    small = jnp.concatenate(
        [depthwise, norm_gain, shifts, attn_bias[:, None], hidden_bias.reshape(depthwise.shape[0], -1)],
        axis=1,
    )
    small = lax.all_gather(small, SHARD, axis=0, tiled=True)
    blocks1 = gather_weights((ffn1_in,), ("y", "x"))
    blocks2 = gather_weights((ffn1_out,), ("x", "y"))
    blocks3 = gather_weights((attn_in, attn_out), ("y", "x"))
    blocks4 = gather_weights((conv_in, conv_out), ("x", "y"))
    blocks5 = gather_weights((ffn2_in,), ("y", "x"))
    blocks6 = gather_weights((ffn2_out,), ("x", "y"))
    holders = lax.axis_size("x") * 2
    width3, width4 = (attn_in.shape[1] // holders, conv_in.shape[1] // holders)
    gathered = (
        whole(blocks1, 0, blocks1.shape[2]),
        whole(blocks2, 0, blocks2.shape[2]),
        whole(blocks3, 0, width3),
        whole(blocks3, width3, blocks3.shape[2] - width3),
        whole(blocks4, 0, width4),
        whole(blocks4, width4, blocks4.shape[2] - width4),
        whole(blocks5, 0, blocks5.shape[2]),
        whole(blocks6, 0, blocks6.shape[2]),
        small[:, :31],
        small[:, 31:37],
        small[:, 37:47],
        small[:, 48:].reshape(-1, 2),
        small[:, 47],
    )
    gains = gathered[9].astype(jnp.float32)
    biases = gathered[10].astype(jnp.float32)
    hidden_biases = gathered[11].astype(jnp.float32)
    output_bias = gathered[12].astype(jnp.float32)
    clips_here, frames_here, feature_width = inputs.shape
    total_rows = clips_here * frames_here
    rim_width = KER - 1
    stream_zero = inputs.astype(jnp.float32).reshape(total_rows, feature_width)
    stream_one, kept_one = feed_forward(
        stream_zero,
        gains[:, 0],
        biases[:, 0],
        gathered[0],
        hidden_biases[:, 0],
        gathered[1],
        biases[:, 6],
    )
    normed_two, pull_two = jax.vjp(layer_norm, stream_one, gains[:, 1], biases[:, 1])
    normed_two = normed_two.astype(jnp.bfloat16)
    projected = matmul(normed_two, gathered[2])
    frame_shape = (clips_here, frames_here, feature_width)
    queries = (projected[:, :feature_width] + biases[:, 8]).astype(jnp.bfloat16)
    values = (projected[:, 2 * feature_width :] + biases[:, 9]).astype(jnp.bfloat16)
    keys_values = jnp.concatenate(
        [projected[:, feature_width : 2 * feature_width].astype(jnp.bfloat16), values], axis=1
    ).reshape(clips_here, frames_here, 2 * feature_width)
    keys_values, order = collect_chunks(keys_values)
    me = lax.axis_index(SEQ)
    where = where_vector(order, me)
    rel_wide = relative_rows(rel_table)
    attended_frames, tops, log_totals = attend(queries, keys_values, where, rel_wide)
    stream_two = stream_one + matmul(attended_frames, gathered[3]) + output_bias
    peaks = jnp.max(tops, axis=0)[:H]
    head_max = jnp.max(lax.all_gather(peaks, ("x", "core", "z", "y")), axis=0)
    qk_scale = jnp.sqrt(clip_threshold / jnp.maximum(head_max, clip_threshold))
    normed_three, pull_three = jax.vjp(layer_norm, stream_two, gains[:, 2], biases[:, 2])
    normed_three = normed_three.astype(jnp.bfloat16)
    mixing = matmul(normed_three, gathered[4])
    gated_half, pull_glu = jax.vjp(gate_linear, mixing)
    gated_half = gated_half.astype(jnp.bfloat16).reshape(frame_shape)
    left_rim = from_behind(gated_half[:, frames_here - rim_width :, :], SEQ, 1)
    padded = jnp.concatenate([left_rim, gated_half], axis=1).astype(jnp.float32)
    tap_weights = gathered[8].astype(jnp.float32)
    convolved = jnp.zeros(frame_shape, jnp.float32)
    for tap_index in range(KER):
        convolved = (
            convolved
            + padded[:, tap_index : tap_index + frames_here, :] * tap_weights[:, tap_index]
        )
    convolved = convolved.reshape(total_rows, feature_width)
    activated, pull_four = jax.vjp(norm_silu, convolved, gains[:, 3], biases[:, 3])
    activated = activated.astype(jnp.bfloat16)
    stream_three = stream_two + matmul(activated, gathered[5])
    stream_four, kept_five = feed_forward(
        stream_three,
        gains[:, 4],
        biases[:, 4],
        gathered[6],
        hidden_biases[:, 1],
        gathered[7],
        biases[:, 7],
    )
    result, pull_final = jax.vjp(layer_norm, stream_four, gains[:, 5], biases[:, 5])
    output = result.astype(jnp.bfloat16).reshape(frame_shape)
    back_weights = gathered
    grad_out = cotangent.astype(jnp.float32).reshape(total_rows, feature_width)
    grad_four, gain_final, shift_final = pull_final(grad_out)
    grad_three, ffn2_grads = feed_back(grad_four, kept_five, back_weights[6], back_weights[7])
    grad_branch = grad_three.astype(jnp.bfloat16)
    grad_conv_out = outer_rows(activated, grad_branch)
    grad_convolved, gain_conv, shift_conv = pull_four(inner_cols(grad_branch, back_weights[5]))
    grad_convolved = grad_convolved.astype(jnp.bfloat16).reshape(frame_shape)
    rim_back = from_behind(grad_convolved[:, :rim_width, :], SEQ, -1)
    padded_back = jnp.concatenate([grad_convolved, rim_back], axis=1).astype(jnp.float32)
    grad_conv_wide = grad_convolved.astype(jnp.float32)
    back_taps = back_weights[8].astype(jnp.float32)
    grad_gated = jnp.zeros(frame_shape, jnp.float32)
    tap_grads = []
    for tap_index in range(KER):
        grad_gated = (
            grad_gated
            + padded_back[:, rim_width - tap_index : rim_width - tap_index + frames_here, :]
            * back_taps[:, tap_index]
        )
        tap_grads.append(
            jnp.sum(padded[:, tap_index : tap_index + frames_here, :] * grad_conv_wide, axis=(0, 1))
        )
    grad_depthwise = jnp.stack(tap_grads, axis=1)
    grad_mixing = pull_glu(grad_gated.reshape(total_rows, feature_width))[0].astype(jnp.bfloat16)
    grad_conv_in = outer_rows(normed_three, grad_mixing)
    grad_normed, gain_three, shift_three = pull_three(inner_cols(grad_mixing, back_weights[4]))
    grad_two = grad_three + grad_normed
    grad_branch = grad_two.astype(jnp.bfloat16)
    grad_attn_out = outer_rows(attended_frames, grad_branch)
    grad_out_bias = jnp.sum(grad_branch.astype(jnp.float32), axis=0)
    grad_attended = inner_cols(grad_branch, back_weights[3]).astype(jnp.bfloat16)
    sides = side_columns(order, me, frames_here)
    grad_q, grad_k, grad_v, grad_band, grad_ends = attend_back(
        queries, keys_values, grad_attended, attended_frames, log_totals, where, rel_wide, sides
    )
    grad_kv = return_chunks(jnp.concatenate([grad_k, grad_v], axis=3))
    grad_kv = grad_kv.reshape(total_rows, 2 * feature_width)
    grad_v = grad_kv[:, feature_width:]
    grad_projected = jnp.concatenate([grad_q, grad_kv], axis=1)
    grad_attn_in = outer_rows(normed_two, grad_projected)
    grad_normed, gain_two, shift_two = pull_two(inner_cols(grad_projected, back_weights[2]))
    grad_one = grad_two + grad_normed
    grad_zero, ffn1_grads = feed_back(grad_one, kept_one, back_weights[0], back_weights[1])
    input_grad = grad_zero.reshape(frame_shape)
    grad_gain = jnp.stack(
        [ffn1_grads[4], gain_two, gain_three, gain_conv, ffn2_grads[4], gain_final], axis=1
    )
    grad_shifts = jnp.stack(
        [
            ffn1_grads[5],
            shift_two,
            shift_three,
            shift_conv,
            ffn2_grads[5],
            shift_final,
            ffn1_grads[3],
            ffn2_grads[3],
            jnp.sum(grad_q.astype(jnp.float32), axis=0),
            jnp.sum(grad_v.astype(jnp.float32), axis=0),
        ],
        axis=1,
    )
    grad_hidden_bias = jnp.stack([ffn1_grads[1], ffn2_grads[1]], axis=1)
    (grad_ffn2_out,) = scatter_grads((ffn2_grads[2],), ("x", "y"))
    (grad_ffn2_in,) = scatter_grads((ffn2_grads[0],), ("y", "x"))
    grad_conv_in, grad_conv_out = scatter_grads((grad_conv_in, grad_conv_out), ("x", "y"))
    grad_attn_in, grad_attn_out = scatter_grads((grad_attn_in, grad_attn_out), ("y", "x"))
    (grad_ffn1_out,) = scatter_grads((ffn1_grads[2],), ("x", "y"))
    (grad_ffn1_in,) = scatter_grads((ffn1_grads[0],), ("y", "x"))
    small_grads = jnp.concatenate(
        [
            grad_depthwise,
            grad_gain,
            grad_shifts,
            grad_out_bias[:, None],
            grad_hidden_bias.reshape(grad_gain.shape[0], -1),
        ],
        axis=1,
    )
    table_flat = jnp.pad(
        table_grad(grad_band, grad_ends).reshape(-1), (0, 5 * grad_gain.shape[0] - REL * HD)
    ).reshape(grad_gain.shape[0], 5)
    small_sum = lax.psum(
        jnp.concatenate([small_grads, table_flat], axis=1), ("x", "core", "z", "y")
    )
    grad_rel_table = small_sum[:, -5:].reshape(-1)[: REL * HD].reshape(REL, HD)
    own_rows = depthwise.shape[0]
    small_own = lax.dynamic_slice_in_dim(
        small_sum, lax.axis_index(SHARD) * own_rows, own_rows, axis=0
    )
    return (
        output,
        input_grad,
        grad_ffn1_in,
        grad_ffn1_out,
        grad_attn_in,
        grad_attn_out,
        grad_conv_in,
        grad_conv_out,
        grad_ffn2_in,
        grad_ffn2_out,
        small_own[:, :31],
        grad_rel_table,
        small_own[:, 31:37],
        small_own[:, 37:47],
        small_own[:, 48:56].reshape(-1, 2),
        small_own[:, 47],
        head_max,
        qk_scale,
    )


def solution(mesh):
    rows = P(SHARD, None)
    tokens = P(SHARD, SEQ, None)
    return jax.shard_map(
        local,
        mesh=refine(mesh),
        in_specs=(tokens, tokens) + (rows,) * 9 + (P(),) + (rows,) * 3 + (P(SHARD), P()),
        out_specs=(tokens, tokens) + (rows,) * 9 + (P(),) + (rows,) * 3 + (P(SHARD), P(), P()),
        check_vma=False,
    )
```

```python
import functools

import jax
import jax.numpy as jnp
from jax import lax
from jax.experimental import pallas as pl
from jax.experimental.layout import Layout, with_layout_constraint
from jax.experimental.pallas import tpu as pltpu
from jax.sharding import Mesh, PartitionSpec as P

H = 16
HD = 64
KER = 31
LEFT = 64
RIGHT = 8
REL = 73
SUB = 128
BAND = 512
VMEM = 56 * 2**20
EPS = 1e-05
SEQ = ("x", "core")
SHARD = ("z", "y")
ALL = ("x", "core", "z", "y")
SWAP = [(0, 1), (1, 0)]


def refine(mesh):
    seq, shard = (mesh.shape["seq"], mesh.shape["shard"])
    devices = mesh.devices.reshape(seq // 2, 2, shard // 2, 2)
    return Mesh(devices, ("x", "core", "z", "y"))


def from_behind(value, axis, steps):
    count = lax.axis_size(axis)
    leading, last = (max(0, -steps), min(count, count - steps))
    return lax.ppermute(value, axis, [(source, source + steps) for source in range(leading, last)])


def own_columns(weight):
    parts = lax.axis_size("x") * 2
    width = weight.shape[1] // parts
    place = lax.axis_index("core") * lax.axis_size("x") + lax.axis_index("x")
    return lax.dynamic_slice_in_dim(weight, place * width, width, axis=1)


def slot(clock, *values):
    return lax.optimization_barrier((values, clock))[0]


def swap(value, axis_name):
    return lax.ppermute(value, axis_name, SWAP)


def spread(value):
    count = lax.axis_size("z")
    return [
        lax.ppermute(value, "z", [(source, (source + step) % count) for source in range(count)])
        for step in range(1, count)
    ]


def place_kernel(moves, count, where, *refs):
    sources, out, sems = refs[:count], refs[count], refs[count + 1]
    x, y, z = where[0], where[1], where[2]
    rows = out.shape[1] // 8
    copies = []
    for source, index, columns, x_place, y_place, z_place in moves(x, y, z):
        row = pl.multiple_of((z_place * 2 + y_place) * rows, rows)
        part = sources[source].at[index]
        if columns is not None:
            part = part.at[:, columns * out.shape[2] : (columns + 1) * out.shape[2]]
        copies.append(pltpu.make_async_copy(part, out.at[x_place, pl.ds(row, rows)], sems.at[len(copies)]))
    for copy in copies:
        copy.start()
    for copy in copies:
        copy.wait()


def mixed_moves(turned, x, y, z):
    for index in range(2):
        z_a = lax.rem(z + 4 - index, 4) if turned else index
        z_b = lax.rem(z + 2 - index, 4) if turned else 2 + index
        yield 0, index, None, x, y, z_a
        yield 1, index, None, x, 1 - y, z_a
        yield 2, index, None, 1 - x, y, z_a
        yield 2, 2 + index, None, 1 - x, 1 - y, z_a
        yield 3, index, None, x, y, z_b
        yield 4, index, None, 1 - x, y, z_b
        yield 5, index, None, x, 1 - y, z_b
        yield 5, 2 + index, None, 1 - x, 1 - y, z_b


def plain_moves(x, y, z):
    for part in range(2):
        for index in range(4):
            yield 0, index, part, part, y, index
            yield 1 + index // 2, index % 2, part, part, 1 - y, index


def place(moves, pieces, width):
    rows = pieces[0].shape[1]
    where = jnp.stack([lax.axis_index(name) for name in ("x", "y", "z")]).astype(jnp.int32)
    return pl.pallas_call(
        functools.partial(place_kernel, moves, len(pieces)),
        grid_spec=pltpu.PrefetchScalarGridSpec(
            num_scalar_prefetch=1,
            grid=(1,),
            in_specs=[pl.BlockSpec(memory_space=pl.ANY)] * len(pieces),
            out_specs=pl.BlockSpec((2, rows * 8, width), lambda step, where: (0, 0, 0)),
            scratch_shapes=[pltpu.SemaphoreType.DMA((16,))],
        ),
        out_shape=jax.ShapeDtypeStruct((2, rows * 8, width), jnp.bfloat16),
        compiler_params=pltpu.CompilerParams(vmem_limit_bytes=VMEM),
        cost_estimate=pl.CostEstimate(flops=0, bytes_accessed=2**23, transcendentals=0),
        name="place",
    )(where, *pieces)


class Gather:
    def __init__(self, parts, turned):
        self.own = jnp.concatenate([own_columns(part) for part in parts], axis=1)
        self.turned = turned

    def over_z(self, clock=()):
        (own,) = slot(clock, self.own)
        if self.turned:
            one, two, three = spread(own)
            self.a0, self.b0 = jnp.stack([own, one]), jnp.stack([two, three])
            return [one, two, three]
        value = lax.all_gather(own, "z", axis=0)
        self.a0, self.b0 = value[:2], value[2:]
        return [value]

    def first(self, clock=()):
        self.a0, self.b0 = slot(clock, self.a0, self.b0)
        self.ya, self.xb = swap(self.a0, "y"), swap(self.b0, "x")
        return [self.ya, self.xb]

    def second(self, clock=()):
        a, b = slot(clock, jnp.concatenate([self.a0, self.ya]), jnp.concatenate([self.b0, self.xb]))
        self.xa, self.yb = swap(a, "x"), swap(b, "y")
        return [self.xa, self.yb]

    def blocks(self, clock=()):
        pieces = slot(clock, self.a0, self.ya, self.xa, self.b0, self.xb, self.yb)
        value = place(functools.partial(mixed_moves, self.turned), pieces, self.own.shape[1])
        value = lax.all_gather(value, "core", axis=0)
        return value.reshape(-1, value.shape[2], value.shape[3])


class PlainGather:
    def __init__(self, part):
        width = part.shape[1] // 2
        self.own = lax.dynamic_slice_in_dim(part, lax.axis_index("core") * width, width, axis=1)

    def over_z(self, clock=()):
        (own,) = slot(clock, self.own)
        self.value = lax.all_gather(own, "z", axis=0)
        return [self.value]

    def half(self, index, clock=()):
        (part,) = slot(clock, self.value[2 * index : 2 * index + 2])
        return [swap(part, "y")]

    def blocks(self, halves, clock=()):
        pieces = slot(clock, self.value, *halves)
        value = place(plain_moves, pieces, self.own.shape[1] // 2)
        value = lax.all_gather(value, "core", axis=0)
        return value.reshape(-1, value.shape[2], value.shape[3])


def gather_weights(parts):
    value = jnp.concatenate([own_columns(part) for part in parts], axis=1)
    rows, width = value.shape
    value = lax.all_gather(lax.all_gather(value, "y", axis=0), "z", axis=0)
    value = lax.all_gather(lax.all_gather(value, "x", axis=0), "core", axis=0)
    return value.reshape(-1, rows * lax.axis_size("z") * 2, width)


def pick(value, index, axis):
    return lax.dynamic_index_in_dim(value, index, axis, keepdims=False)


def add(left_op, right_op):
    return (left_op.astype(F32) + right_op.astype(F32)).astype(BF16)


class Scatter:
    def __init__(self, value):
        self.value = value.reshape(2, value.shape[0] // 2, *value.shape[1:])

    def over_core(self, clock=()):
        (value,) = slot(clock, self.value)
        value = lax.psum_scatter(value, "core", scatter_dimension=0, tiled=True)[0]
        self.value = with_layout_constraint(value, Layout(major_to_minor=tuple(range(5))))
        return [self.value]

    def first(self, clock=()):
        x, y = lax.axis_index("x"), lax.axis_index("y")
        value = self.value
        a, b = slot(clock, pick(value[:, :, :2], 1 - x, 0), pick(value[:, :, 2:], 1 - y, 1))
        self.got_a, self.got_b = swap(a, "x"), swap(b, "y")
        return [self.got_a, self.got_b]

    def second(self, clock=()):
        x, y = lax.axis_index("x"), lax.axis_index("y")
        a = add(pick(self.value[:, :, :2], x, 0), self.got_a)
        b = add(pick(self.value[:, :, 2:], y, 1), self.got_b)
        self.a, self.b = pick(a, y, 0), pick(b, x, 0)
        sent_a, sent_b = slot(clock, pick(a, 1 - y, 0), pick(b, 1 - x, 0))
        self.got_a, self.got_b = swap(sent_a, "y"), swap(sent_b, "x")
        return [self.got_a, self.got_b]

    def last(self):
        value = jnp.concatenate([add(self.a, self.got_a), add(self.b, self.got_b)])
        return lax.psum_scatter(value, "z", scatter_dimension=0, tiled=True)[0]


def scatter_grads(value):
    value = value.reshape(2, value.shape[0] // 2, *value.shape[1:])
    value = lax.psum_scatter(value, "core", scatter_dimension=0, tiled=True)[0]
    value = lax.psum_scatter(value, "x", scatter_dimension=0, tiled=True)[0]
    value = lax.psum_scatter(value, "y", scatter_dimension=0, tiled=True)[0]
    return lax.psum_scatter(value, "z", scatter_dimension=0, tiled=True)[0]


def share_columns(values):
    return lax.all_gather(jnp.concatenate(values, axis=1), ("core", "x"), axis=0)


def unfold(value, start, stop):
    part = jnp.transpose(value[:, :, start:stop], (1, 0, 2))
    return part.reshape(part.shape[0], -1).astype(F32)


def combine_all(value, peaks):
    if lax.axis_size("x") != 2 or lax.axis_size("z") != 4:
        return lax.psum(value, ALL), jnp.max(lax.all_gather(peaks, ALL), axis=0)
    rows = value.shape[0]
    both = jnp.concatenate([value, peaks])
    top = jnp.arange(both.shape[0])[:, None] >= rows
    pairs = {"core": [SWAP], "x": [SWAP], "y": [SWAP]}
    pairs["z"] = [[(0, 1), (1, 0), (2, 3), (3, 2)], [(0, 2), (2, 0), (1, 3), (3, 1)]]
    for name in ("core", "x", "y", "z"):
        for moves in pairs[name]:
            got = lax.ppermute(both, name, moves)
            both = jnp.where(top, jnp.maximum(both, got), both + got)
    return both[:rows], both[rows:]


def dot_tt(left_op, right_op):
    return lax.dot_general(left_op, right_op, (((1,), (1,)), ((), ())), preferred_element_type=jnp.float32)


def dot_nn(left_op, right_op):
    return lax.dot_general(left_op, right_op, (((1,), (0,)), ((), ())), preferred_element_type=jnp.float32)


def dot_tn(left_op, right_op):
    return lax.dot_general(left_op, right_op, (((0,), (0,)), ((), ())), preferred_element_type=jnp.float32)


def relative_rows(rel_table):
    distance = jnp.clip(jnp.arange(BAND, dtype=jnp.int32) - BAND // 2, -LEFT, RIGHT) + LEFT
    rows = jnp.take(rel_table, distance, axis=0)
    return jnp.concatenate([rows, rows], axis=1)


def side_columns(order, me, frames):
    groups = frames // SUB
    chunk = jnp.repeat(order, frames)
    block = chunk * groups + jnp.tile(jnp.arange(frames, dtype=jnp.int32) // SUB, order.shape[0])
    columns = []
    for group in range(groups):
        place = me * groups + group
        columns += [block < place - 1, block > place + 1]
    marks = jnp.stack(columns, axis=1).astype(jnp.bfloat16)
    return jnp.pad(marks, ((0, 0), (0, 128 - marks.shape[1])))


def place_bias(scores, raw, base, off, where, me, frames, chunks):
    groups = frames // SUB
    left, right = base[:, :1] + off, base[:, BAND - 1 :] + off
    for group in range(groups):
        rows = slice(group * SUB, (group + 1) * SUB)
        own = me * groups + group
        for chunk in range(chunks):
            for part in range(groups):
                block = where[chunk] * groups + part
                col = (chunk * groups + part) * SUB
                side = jnp.where(block <= own, left[rows], right[rows])
                scores[rows, col : col + SUB] = raw[rows, col : col + SUB] + side
        band = pltpu.roll(base[rows] + off[rows], BAND - SUB, 1, stride=1, stride_axis=0)
        for step in (-1, 0, 1):
            chunk_step = (group + step) // groups
            part = (group + step) % groups
            place = where[chunks + 1 + chunk_step]
            col = pl.multiple_of((jnp.maximum(place, 0) * groups + part) * SUB, SUB)
            side = right[rows] if step > 0 else left[rows]
            piece = band[:, (step + 1) * SUB : (step + 2) * SUB] - side
            held = scores[rows, pl.ds(col, SUB)]
            scores[rows, pl.ds(col, SUB)] = held + jnp.where(place >= 0, piece, 0.0)


def attend_kernel(frames, chunks, where, *refs):
    q_ref, rel_ref, *refs = refs
    kv_refs, refs = refs[:chunks], refs[chunks:]
    o_ref, top_ref, log_ref, scores = refs[-4:]
    pair = pl.program_id(0)
    me = where[chunks + 3]
    query = q_ref[...]
    keys = jnp.concatenate([ref[0] for ref in kv_refs])
    values = jnp.concatenate([ref[1] for ref in kv_refs])
    lane = lax.broadcasted_iota(jnp.int32, (frames, 2 * HD), 1)
    outs = []
    for half in range(2):
        inside = (lane // HD) == half
        here = lane == pair * 2 + half
        query_half = jnp.where(inside, query, 0) * jnp.bfloat16(HD ** (-0.5))
        base = dot_tt(query_half, rel_ref[...])
        held = scores.at[half]
        zero = jnp.zeros((frames, 1), jnp.float32)
        place_bias(held, dot_tt(query_half, keys), base, zero, where, me, frames, chunks)
        full = held[...]
        top = jnp.max(full, axis=1, keepdims=True)
        weights = jnp.exp(full - top)
        total = jnp.sum(weights, axis=1, keepdims=True)
        outs.append(dot_nn(weights.astype(jnp.bfloat16), values) * (1.0 / total))
        top_ref[...] = jnp.where(here, top, top_ref[...])
        log_ref[...] = jnp.where(here, top + jnp.log(total), log_ref[...])
    o_ref[...] = jnp.where(lane < HD, outs[0], outs[1]).astype(o_ref.dtype)


def attend_back_kernel(frames, chunks, first, where, *refs):
    q_ref, do_ref, o_ref, log_ref, rel_ref, side_ref, ends_ref, flip_ref, *refs = refs
    kv_refs, refs = refs[:chunks], refs[chunks:]
    if not first:
        gt_in, ge_in, _, *refs = refs
    dq_ref, gt_ref, ge_ref, *refs = refs
    dkv_refs, (scores, window) = refs[:chunks], refs[chunks:]
    pair = pl.program_id(0)
    me = where[chunks + 3]
    groups = frames // SUB
    query, grad = q_ref[...], do_ref[...]
    keys = jnp.concatenate([ref[0] for ref in kv_refs])
    values = jnp.concatenate([ref[1] for ref in kv_refs])
    keys_side = jnp.concatenate([keys, side_ref[...]], axis=1)
    lane = lax.broadcasted_iota(jnp.int32, (frames, 2 * HD), 1)
    product = grad.astype(jnp.float32) * o_ref[...].astype(jnp.float32)

    @pl.when(pair == 0)
    def _():
        gt_ref[...] = jnp.zeros_like(gt_ref) if first else gt_in[...]
        ge_ref[...] = jnp.zeros_like(ge_ref) if first else ge_in[...]

    parts = []
    for half in range(2):
        inside = (lane // HD) == half
        query_half = jnp.where(inside, query, 0) * jnp.bfloat16(HD ** (-0.5))
        grad_half = jnp.where(inside, grad, 0)
        base = dot_tt(query_half, rel_ref[...])
        held_scores = scores.at[half]
        log_total = jnp.sum(jnp.where(lane == pair * 2 + half, log_ref[...], 0.0), axis=1, keepdims=True)
        place_bias(held_scores, dot_tt(query_half, keys), base, -log_total, where, me, frames, chunks)
        delta = jnp.sum(jnp.where(inside, product, 0.0), axis=1, keepdims=True)
        weights = jnp.exp(held_scores[...])
        grad_weights = dot_tt(grad_half, values)
        grad_scores = (weights * (grad_weights - delta)).astype(jnp.bfloat16)
        window[half] = grad_scores
        grad_values = dot_tn(weights.astype(jnp.bfloat16), grad)
        grad_keys = dot_tn(grad_scores, query) * HD ** (-0.5)
        wide = dot_nn(grad_scores, keys_side)
        grad_query = wide[:, : 2 * HD]
        pieces = []
        for group in range(groups):
            rows = slice(group * SUB, (group + 1) * SUB)
            bands = []
            for step in (-1, 0, 1):
                chunk_step = (group + step) // groups
                part = (group + step) % groups
                place = where[chunks + 1 + chunk_step]
                col = pl.multiple_of((jnp.maximum(place, 0) * groups + part) * SUB, SUB)
                held = window[half, rows, pl.ds(col, SUB)]
                bands.append(jnp.where(place >= 0, held, jnp.zeros_like(held)))
            flipped = dot_nn(flip_ref[...], jnp.concatenate(bands, axis=1))
            flipped = jnp.concatenate([flipped, jnp.zeros((SUB, SUB), jnp.float32)], axis=1)
            turned = pltpu.roll(flipped, 1, 1, stride=1, stride_axis=0).astype(jnp.bfloat16)
            turned = dot_nn(flip_ref[...], turned).astype(jnp.bfloat16)
            left = wide[rows, 2 * HD + 2 * group : 2 * HD + 2 * group + 1]
            right = wide[rows, 2 * HD + 2 * group + 1 : 2 * HD + 2 * group + 2]
            pieces.append(
                grad_query[rows] + dot_nn(turned, rel_ref[...]) + left * ends_ref[:1] + right * ends_ref[1:2]
            )
            gt_ref[...] += dot_tn(turned, query_half[rows])
            query_wide = query_half[rows].astype(jnp.float32)
            ge_ref[0:1] += jnp.sum(left * query_wide, axis=0, keepdims=True)
            ge_ref[1:2] += jnp.sum(right * query_wide, axis=0, keepdims=True)
        parts.append((jnp.concatenate(pieces, axis=0) * HD ** (-0.5), grad_keys, grad_values))
    dq_ref[...] = jnp.where(lane < HD, parts[0][0], parts[1][0]).astype(dq_ref.dtype)
    lane_keys = lax.broadcasted_iota(jnp.int32, (chunks * frames, 2 * HD), 1) < HD
    for place in range(2):
        merged = jnp.where(lane_keys, parts[0][1 + place], parts[1][1 + place]).astype(jnp.bfloat16)
        for chunk in range(chunks):
            dkv_refs[chunk][place] = merged[chunk * frames : (chunk + 1) * frames]


def where_vector(order, me):
    places = []
    for step in (-1, 0, 1):
        match = order == me + step
        places.append(jnp.where(jnp.any(match), jnp.argmax(match), -1))
    return jnp.concatenate([order, jnp.stack(places), me[None]]).astype(jnp.int32)


def attend(query, clip, clips, chunks_kv, where, rel_wide, before=None):
    chunks = len(chunks_kv)
    _, frames, width = chunks_kv[0].shape
    pairs = width // (2 * HD)
    rows = pl.BlockSpec((frames, 2 * HD), lambda pair, where: (clip, pair))
    stats = pl.BlockSpec((frames, 128), lambda pair, where: (clip, 0))
    both = pl.BlockSpec((2, frames, 2 * HD), lambda pair, where: (0, 0, pair))
    args = [query, rel_wide, *chunks_kv]
    in_specs = [rows, pl.BlockSpec((BAND, 2 * HD), lambda pair, where: (0, 0))] + [both] * chunks
    aliases = {}
    if before is not None:
        aliases = {len(args) + 1 + index: index for index in range(3)}
        args += list(before)
        in_specs += [pl.BlockSpec(memory_space=pl.ANY)] * 3
    size = frames * chunks * frames * width
    return pl.pallas_call(
        functools.partial(attend_kernel, frames, chunks),
        grid_spec=pltpu.PrefetchScalarGridSpec(
            num_scalar_prefetch=1,
            grid=(pairs,),
            in_specs=in_specs,
            out_specs=[rows, stats, stats],
            scratch_shapes=[pltpu.VMEM((2, frames, chunks * frames), jnp.float32)],
        ),
        out_shape=[
            jax.ShapeDtypeStruct((clips * frames, width), jnp.bfloat16),
            jax.ShapeDtypeStruct((clips * frames, 128), jnp.float32),
            jax.ShapeDtypeStruct((clips * frames, 128), jnp.float32),
        ],
        input_output_aliases=aliases,
        compiler_params=pltpu.CompilerParams(vmem_limit_bytes=VMEM),
        cost_estimate=pl.CostEstimate(flops=80 * size, bytes_accessed=2**22, transcendentals=size // HD),
        name="attend",
    )(where, *args)


def attend_back(query, clip, clips, chunks_kv, grad, attended, log_totals, where, rel_wide, sides, before=None):
    chunks = len(chunks_kv)
    _, frames, width = chunks_kv[0].shape
    pairs = width // (2 * HD)
    rows = pl.BlockSpec((frames, 2 * HD), lambda pair, where: (clip, pair))
    stats = pl.BlockSpec((frames, 128), lambda pair, where: (clip, 0))
    both = pl.BlockSpec((2, frames, 2 * HD), lambda pair, where: (0, 0, pair))
    fixed = lambda shape: pl.BlockSpec(shape, lambda pair, where: (0, 0))
    ends = jnp.concatenate([rel_wide[:1], rel_wide[-1:], jnp.zeros((6, 2 * HD), rel_wide.dtype)]).astype(jnp.float32)
    flip = jnp.eye(SUB, dtype=jnp.bfloat16)[::-1]
    args = [query, grad, attended, log_totals, rel_wide, sides, ends, flip, *chunks_kv]
    in_specs = [
        rows, rows, rows, stats, fixed((BAND, 2 * HD)), fixed((chunks * frames, 128)),
        fixed((8, 2 * HD)), fixed((SUB, SUB)),
    ] + [both] * chunks
    aliases = {}
    if before is not None:
        grad_query, band, table_ends = before
        args += [band, table_ends, grad_query]
        in_specs += [fixed((BAND, 2 * HD)), fixed((8, 2 * HD)), pl.BlockSpec(memory_space=pl.ANY)]
        aliases = {len(args): 0}
    size = frames * chunks * frames * width
    result = pl.pallas_call(
        functools.partial(attend_back_kernel, frames, chunks, before is None),
        grid_spec=pltpu.PrefetchScalarGridSpec(
            num_scalar_prefetch=1,
            grid=(pairs,),
            in_specs=in_specs,
            out_specs=[rows, fixed((BAND, 2 * HD)), fixed((8, 2 * HD))] + [both] * chunks,
            scratch_shapes=[
                pltpu.VMEM((2, frames, chunks * frames), jnp.float32),
                pltpu.VMEM((2, frames, chunks * frames), jnp.bfloat16),
            ],
        ),
        out_shape=[
            jax.ShapeDtypeStruct((clips * frames, width), jnp.bfloat16),
            jax.ShapeDtypeStruct((BAND, 2 * HD), jnp.float32),
            jax.ShapeDtypeStruct((8, 2 * HD), jnp.float32),
        ]
        + [jax.ShapeDtypeStruct((2, frames, width), jnp.bfloat16)] * chunks,
        input_output_aliases=aliases,
        compiler_params=pltpu.CompilerParams(vmem_limit_bytes=VMEM),
        cost_estimate=pl.CostEstimate(flops=160 * size, bytes_accessed=2**23, transcendentals=size // HD),
        name="attend_back",
    )(where, *args)
    return result[:3], result[3:]


def table_grad(grad_band, grad_ends):
    distance = jnp.clip(jnp.arange(BAND, dtype=jnp.int32) - BAND // 2, -LEFT, RIGHT) + LEFT
    both = grad_band[:, :HD] + grad_band[:, HD:]
    ends = grad_ends[:2, :HD] + grad_ends[:2, HD:]
    first = BAND // 2 - LEFT
    middle = both[first : first + REL]
    low = jnp.sum(both[:first], axis=0) + ends[0]
    high = jnp.sum(both[first + REL :], axis=0) + ends[1]
    return jnp.concatenate([middle[:1] + low, middle[1:-1], middle[-1:] + high])


def spec(shape, index):
    return pl.BlockSpec(shape, index)


def full(shape):
    return pl.BlockSpec(shape, lambda step: (0,) * len(shape))


def call(kernel, steps, in_specs, out_specs, out_shape, scratch, args, name, macs):
    read = sum(arg.size * arg.dtype.itemsize for arg in args)
    return pl.pallas_call(
        kernel,
        grid=(steps,),
        in_specs=in_specs,
        out_specs=out_specs,
        out_shape=out_shape,
        scratch_shapes=scratch,
        compiler_params=pltpu.CompilerParams(vmem_limit_bytes=VMEM),
        cost_estimate=pl.CostEstimate(flops=2 * macs, bytes_accessed=read, transcendentals=0),
        name=name,
    )(*args)


def struct(shape, dtype):
    return jax.ShapeDtypeStruct(shape, dtype)


F32 = jnp.float32
BF16 = jnp.bfloat16


def norm_parts(stream):
    average = jnp.mean(stream, axis=-1, keepdims=True)
    centred = stream - average
    variance = jnp.mean(centred * centred, axis=-1, keepdims=True)
    scale = lax.rsqrt(variance + EPS)
    return centred * scale, scale


def norm_back(grad, unit, scale, gain):
    scaled = grad * gain
    first = jnp.mean(scaled, axis=-1, keepdims=True)
    second = jnp.mean(scaled * unit, axis=-1, keepdims=True)
    return (
        scale * (scaled - first - unit * second),
        jnp.sum(grad * unit, axis=0, keepdims=True),
        jnp.sum(grad, axis=0, keepdims=True),
    )


def store_rows(ref, cols, value):
    _, _, depth, rows, _ = ref.shape
    for z in range(depth):
        for y in range(2):
            start = (z * 2 + y) * rows
            ref[0, y, z, :, cols] = value[start : start + rows].astype(BF16)


def ffn_kernel(steps, last, x_ref, rows_ref, bias_ref, win_ref, wout_ref, *refs):
    if last:
        cot_ref, ends_ref, out_ref, grad_ref, sums_ref, normed_ref, hidden_ref, stream_ref, total = refs
    else:
        stream_ref, normed_ref, hidden_ref, total = refs
    step = pl.program_id(0)
    piece = wout_ref.shape[2]

    @pl.when(step == 0)
    def _():
        unit, _ = norm_parts(x_ref[...].astype(F32))
        normed_ref[...] = (unit * rows_ref[0:1] + rows_ref[1:2]).astype(BF16)
        total[...] = jnp.zeros_like(total)

    hidden = dot_nn(normed_ref[...], win_ref[0]) + bias_ref[0:1]
    hidden_ref[...] = hidden.astype(BF16)
    active = (hidden * jax.nn.sigmoid(hidden)).astype(BF16)
    for part in range(steps):
        cols = slice(part * piece, (part + 1) * piece)
        total[:, cols] += dot_nn(active, wout_ref[part])

    @pl.when(step == steps - 1)
    def _():
        stream = x_ref[...].astype(F32) + 0.5 * (total[...] + rows_ref[2:3])
        stream_ref[...] = stream
        if last:
            unit, scale = norm_parts(stream)
            out_ref[...] = (unit * ends_ref[0:1] + ends_ref[1:2]).astype(BF16)
            grad, gain_row, shift_row = norm_back(cot_ref[...].astype(F32), unit, scale, ends_ref[0:1])
            grad_ref[...] = grad
            sums_ref[...] = jnp.zeros_like(sums_ref)
            sums_ref[0:1] = gain_row
            sums_ref[1:2] = shift_row


def ffn(x, rows, bias, win, wout, last=None):
    tokens, width = x.shape
    steps, _, hidden = win.shape
    args = [x, rows, bias, win, wout]
    in_specs = [
        full((tokens, width)),
        full(rows.shape),
        spec((8, hidden), lambda step: (0, step)),
        spec((1, width, hidden), lambda step: (step, 0, 0)),
        spec((steps, hidden, wout.shape[2]), lambda step: (0, step, 0)),
    ]
    saved_specs = [full((tokens, width)), spec((tokens, hidden), lambda step: (0, step))]
    saved_shapes = [struct((tokens, width), BF16), struct((tokens, hidden * steps), BF16)]
    stream_spec, stream_shape = [full((tokens, width))], [struct((tokens, width), F32)]
    if last is None:
        out_specs, out_shape = stream_spec + saved_specs, stream_shape + saved_shapes
    else:
        args += list(last)
        in_specs += [full((tokens, width)), full(last[1].shape)]
        out_specs = [full((tokens, width)), full((tokens, width)), full((8, width))] + saved_specs + stream_spec
        out_shape = [struct((tokens, width), BF16), struct((tokens, width), F32), struct((8, width), F32)]
        out_shape += saved_shapes + stream_shape
    return call(
        functools.partial(ffn_kernel, steps, last is not None),
        steps, in_specs, out_specs, out_shape, [pltpu.VMEM((tokens, width), F32)], args, "ffn",
        2 * tokens * width * hidden * steps,
    )


def ffn_out_kernel(steps, grad_ref, hidden_ref, gout_ref, branch):
    @pl.when(pl.program_id(0) == 0)
    def _():
        branch[...] = (0.5 * grad_ref[...]).astype(BF16)

    hidden = hidden_ref[...].astype(F32)
    active = (hidden * jax.nn.sigmoid(hidden)).astype(BF16)
    wide = dot_tn(active, branch[...])
    piece = wide.shape[1] // steps
    for part in range(steps):
        store_rows(gout_ref.at[part : part + 1], slice(None), wide[:, part * piece : (part + 1) * piece])


def ffn_out_grad(grad, hidden, steps, depth):
    tokens, width = grad.shape
    block = hidden.shape[1] // steps
    rows_out = hidden.shape[1] // depth // 2
    piece = width // steps
    return call(
        functools.partial(ffn_out_kernel, steps),
        steps,
        [full((tokens, width)), spec((tokens, block), lambda step: (0, step))],
        [spec((steps, 2, block // rows_out // 2, rows_out, piece), lambda step: (0, 0, step, 0, 0))],
        [struct((steps, 2, depth, rows_out, piece), BF16)],
        [pltpu.VMEM((tokens, width), BF16)],
        [grad, hidden],
        "ffn_out_grad",
        tokens * width * block * steps,
    )[0]


def ffn_back_kernel(steps, with_out, grad_ref, x_ref, rows_ref, normed_ref, hidden_ref, win_ref, wout_ref, *refs):
    if with_out:
        gout_ref, *refs = refs
    gx_ref, gin_ref, sums_ref, gbias_ref, branch, total = refs
    step = pl.program_id(0)
    piece = wout_ref.shape[2]

    @pl.when(step == 0)
    def _():
        half = (0.5 * grad_ref[...]).astype(BF16)
        branch[...] = half
        total[...] = jnp.zeros_like(total)
        sums_ref[...] = jnp.zeros_like(sums_ref)
        sums_ref[2:3] = jnp.sum(half.astype(F32), axis=0, keepdims=True)

    grad_active = dot_tt(branch[:, :piece], wout_ref[0])
    for part in range(1, steps):
        grad_active += dot_tt(branch[:, part * piece : (part + 1) * piece], wout_ref[part])
    hidden = hidden_ref[...].astype(F32)
    gate = jax.nn.sigmoid(hidden)
    active = hidden * gate
    grad_hidden = (grad_active * (gate + active * (1.0 - gate))).astype(BF16)
    if with_out:
        wide = dot_tn(active.astype(BF16), branch[...])
        for part in range(steps):
            store_rows(gout_ref.at[part : part + 1], slice(None), wide[:, part * piece : (part + 1) * piece])
    store_rows(gin_ref, slice(None), dot_tn(normed_ref[...], grad_hidden))
    gbias_ref[...] = jnp.broadcast_to(
        jnp.sum(grad_hidden.astype(F32), axis=0, keepdims=True), gbias_ref.shape
    )
    total[...] += dot_tt(grad_hidden, win_ref[0])

    @pl.when(step == steps - 1)
    def _():
        unit, scale = norm_parts(x_ref[...].astype(F32))
        grad, gain_row, shift_row = norm_back(total[...], unit, scale, rows_ref[0:1])
        gx_ref[...] = grad_ref[...] + grad
        sums_ref[0:1] = gain_row
        sums_ref[1:2] = shift_row


def ffn_back(grad, x, rows, normed, hidden, win, wout, depth, with_out):
    tokens, width = x.shape
    steps, _, block = win.shape
    piece = wout.shape[2]
    rows_in, rows_out = width // depth // 2, wout.shape[1] // depth // 2
    gin_shape = (steps, 2, depth, rows_in, block)
    gout_shape = (steps, 2, depth, rows_out, piece)
    gin_spec = spec((1,) + gin_shape[1:], lambda step: (step, 0, 0, 0, 0))
    gout_spec = spec((steps, 2, block // rows_out // 2, rows_out, piece), lambda step: (0, 0, step, 0, 0))
    win_spec = spec((1, width, block), lambda step: (step, 0, 0))
    wout_spec = spec((steps, block, piece), lambda step: (0, step, 0))
    result = call(
        functools.partial(ffn_back_kernel, steps, with_out),
        steps,
        [
            full((tokens, width)), full((tokens, width)), full(rows.shape), full((tokens, width)),
            spec((tokens, block), lambda step: (0, step)), win_spec, wout_spec,
        ],
        [gout_spec] * with_out
        + [full((tokens, width)), gin_spec, full((8, width)), spec((8, block), lambda step: (0, step))],
        [struct(gout_shape, BF16)] * with_out
        + [
            struct((tokens, width), F32), struct(gin_shape, BF16),
            struct((8, width), F32), struct((8, block * steps), F32),
        ],
        [pltpu.VMEM((tokens, width), BF16), pltpu.VMEM((tokens, width), F32)],
        [grad, x, rows, normed, hidden, win, wout],
        "ffn_back",
        (3 + with_out) * tokens * width * block * steps,
    )
    return result if with_out else [None, *result]


def project_kernel(frames, x_ref, rows_ref, bias_ref, wq_ref, wk_ref, wv_ref, normed_ref, q_ref, *kv_refs):
    @pl.when(pl.program_id(0) == 0)
    def _():
        unit, _ = norm_parts(x_ref[...])
        normed_ref[...] = (unit * rows_ref[0:1] + rows_ref[1:2]).astype(BF16)

    normed = normed_ref[...]
    q_ref[...] = (dot_nn(normed, wq_ref[0]) + bias_ref[0:1]).astype(BF16)
    keys = dot_nn(normed, wk_ref[0]).astype(BF16)
    values = (dot_nn(normed, wv_ref[0]) + bias_ref[1:2]).astype(BF16)
    for clip, kv_ref in enumerate(kv_refs):
        kv_ref[0] = keys[clip * frames : (clip + 1) * frames]
        kv_ref[1] = values[clip * frames : (clip + 1) * frames]


def column(width, piece, place):
    return spec((1, width, piece), lambda step: (step, 0, place))


def project(x, rows, bias, blocks, frames):
    tokens, width = x.shape
    steps = blocks.shape[0]
    piece = width // steps
    clips = tokens // frames
    col = spec((tokens, piece), lambda step: (0, step))
    result = call(
        functools.partial(project_kernel, frames),
        steps,
        [full((tokens, width)), full(rows.shape), spec((8, piece), lambda step: (0, step))]
        + [column(width, piece, place) for place in range(3)],
        [full((tokens, width)), col] + [spec((2, frames, piece), lambda step: (0, 0, step))] * clips,
        [struct((tokens, width), BF16), struct((tokens, width), BF16)]
        + [struct((2, frames, width), BF16)] * clips,
        [],
        [x, rows, bias, blocks, blocks, blocks],
        "project",
        3 * tokens * width * width,
    )
    return result[0], result[1], result[2:]


def mix_kernel(
    steps, att_ref, x_ref, rows_ref, wo_ref, wa_ref, wb_ref, stream_ref, normed_ref, mix_ref, gated_ref
):
    piece = wo_ref.shape[2]

    @pl.when(pl.program_id(0) == 0)
    def _():
        for part in range(steps):
            cols = slice(part * piece, (part + 1) * piece)
            stream_ref[:, cols] = x_ref[:, cols] + dot_nn(att_ref[...], wo_ref[part]) + rows_ref[2:3, cols]
        unit, _ = norm_parts(stream_ref[...])
        normed_ref[...] = (unit * rows_ref[0:1] + rows_ref[1:2]).astype(BF16)

    normed = normed_ref[...]
    left = dot_nn(normed, wa_ref[0])
    right = dot_nn(normed, wb_ref[0])
    mix_ref[0] = left.astype(BF16)
    mix_ref[1] = right.astype(BF16)
    gated_ref[...] = (left * jax.nn.sigmoid(right)).astype(BF16)


def mix(attended, x, rows, attn_blocks, conv_blocks):
    tokens, width = x.shape
    steps = attn_blocks.shape[0]
    piece = width // steps
    col = spec((tokens, piece), lambda step: (0, step))
    return call(
        functools.partial(mix_kernel, steps),
        steps,
        [
            full((tokens, width)), full((tokens, width)), full(rows.shape),
            spec((steps, width, piece), lambda step: (0, 0, 3)),
            column(width, piece, 0), column(width, piece, 1),
        ],
        [full((tokens, width)), full((tokens, width)), spec((2, tokens, piece), lambda step: (0, 0, step)), col],
        [
            struct((tokens, width), F32), struct((tokens, width), BF16),
            struct((2, tokens, width), BF16), struct((tokens, width), BF16),
        ],
        [],
        [attended, x, rows, attn_blocks, conv_blocks, conv_blocks],
        "mix",
        3 * tokens * width * width,
    )


RIM = 32


def windows(padded, frames):
    for rest in range(8):
        most = RIM if rest == 0 else RIM - 8
        shifted = padded[rest : rest + most + frames]
        for lead in range(0, most + 1, 8):
            yield rest + lead, shifted[lead : lead + frames]


def convolve_kernel(
    steps, frames, gated_ref, rim_ref, taps_ref, x_ref, rows_ref, wo_ref, stream_ref, conv_ref, padded, held
):
    step = pl.program_id(0)
    piece = wo_ref.shape[2]
    tokens = gated_ref.shape[0]
    for clip in range(tokens // frames):
        padded[:RIM] = rim_ref[clip * RIM : (clip + 1) * RIM].astype(F32)
        padded[RIM:] = gated_ref[clip * frames : (clip + 1) * frames].astype(F32)
        result = jnp.zeros((frames, piece), F32)
        for offset, window in windows(padded, frames):
            if 2 <= offset <= KER + 1:
                result = result + window * taps_ref[offset - 2 : offset - 1]
        conv_ref[clip * frames : (clip + 1) * frames] = result
        held[step, clip * frames : (clip + 1) * frames] = result

    @pl.when(step == steps - 1)
    def _():
        stream = jnp.concatenate([held[part] for part in range(steps)], axis=1)
        unit, _ = norm_parts(stream)
        normed = unit * rows_ref[0:1] + rows_ref[1:2]
        active = (normed * jax.nn.sigmoid(normed)).astype(BF16)
        for part in range(steps):
            cols = slice(part * piece, (part + 1) * piece)
            stream_ref[:, cols] = x_ref[:, cols] + dot_nn(active, wo_ref[part])


def convolve(gated, rim, taps, x, rows, conv_blocks, frames):
    tokens, width = x.shape
    steps = conv_blocks.shape[0]
    piece = width // steps
    col = lambda rows_here: spec((rows_here, piece), lambda step: (0, step))
    return call(
        functools.partial(convolve_kernel, steps, frames),
        steps,
        [
            col(tokens), col(rim.shape[0]), col(taps.shape[0]), full((tokens, width)), full(rows.shape),
            spec((steps, width, piece), lambda step: (0, 0, 2)),
        ],
        [full((tokens, width)), col(tokens)],
        [struct((tokens, width), F32), struct((tokens, width), F32)],
        [pltpu.VMEM((RIM + frames, piece), F32), pltpu.VMEM((steps, tokens, piece), F32)],
        [gated, rim, taps, x, rows, conv_blocks],
        "convolve",
        tokens * width * width,
    )


def norm_silu_back_kernel(steps, grad_ref, conv_ref, rows_ref, wo_ref, gconv_ref, gw_ref, sums_ref):
    piece = wo_ref.shape[2]
    branch = grad_ref[...].astype(BF16)
    unit, scale = norm_parts(conv_ref[...])
    normed = unit * rows_ref[0:1] + rows_ref[1:2]
    gate = jax.nn.sigmoid(normed)
    active = normed * gate
    slope = gate + active * (1.0 - gate)
    active = active.astype(BF16)
    grad_active = dot_tt(branch[:, :piece], wo_ref[0])
    for part in range(1, steps):
        grad_active += dot_tt(branch[:, part * piece : (part + 1) * piece], wo_ref[part])
    grad, gain_row, shift_row = norm_back(grad_active * slope, unit, scale, rows_ref[0:1])
    gconv_ref[...] = grad.astype(BF16)
    sums_ref[...] = jnp.zeros_like(sums_ref)
    sums_ref[0:1] = gain_row
    sums_ref[1:2] = shift_row
    for part in range(steps):
        gw_ref[part] = dot_tn(active, branch[:, part * piece : (part + 1) * piece]).astype(BF16)


def norm_silu_back(grad, convolved, rows, conv_blocks):
    tokens, width = grad.shape
    steps = conv_blocks.shape[0]
    piece = width // steps
    return call(
        functools.partial(norm_silu_back_kernel, steps),
        1,
        [
            full((tokens, width)), full((tokens, width)), full(rows.shape),
            spec((steps, width, piece), lambda step: (0, 0, 2)),
        ],
        [full((tokens, width)), full((steps, width, piece)), full((8, width))],
        [struct((tokens, width), BF16), struct((steps, width, piece), BF16), struct((8, width), F32)],
        [],
        [grad, convolved, rows, conv_blocks],
        "norm_silu_back",
        2 * tokens * width * width,
    )


def conv_back_kernel(
    steps, frames, gconv_ref, next_ref, gated_ref, rim_ref, taps_ref, mix_ref, normed_ref, wa_ref, wb_ref,
    x_ref, grad_ref, rows_ref, pass_ref, gx_ref, gw_ref, gtaps_ref, sums_ref, padded, total
):
    step = pl.program_id(0)
    piece = wa_ref.shape[2]
    tokens = gated_ref.shape[0]

    @pl.when(step == 0)
    def _():
        total[...] = jnp.zeros_like(total)

    gtaps_ref[...] = jnp.zeros_like(gtaps_ref)
    halves = []
    for clip in range(tokens // frames):
        rows = slice(clip * frames, (clip + 1) * frames)
        grad_conv = gconv_ref[rows].astype(F32)
        padded[:RIM] = rim_ref[clip * RIM : (clip + 1) * RIM].astype(F32)
        padded[RIM:] = gated_ref[rows].astype(F32)
        for offset, window in windows(padded, frames):
            if 2 <= offset <= KER + 1:
                gtaps_ref[offset - 2 : offset - 1] += jnp.sum(window * grad_conv, axis=0, keepdims=True)
        padded[:frames] = grad_conv
        padded[frames:] = next_ref[clip * RIM : (clip + 1) * RIM].astype(F32)
        result = jnp.zeros((frames, piece), F32)
        for offset, window in windows(padded, frames):
            if offset <= KER - 1:
                result = result + window * taps_ref[KER - 1 - offset : KER - offset]
        left = mix_ref[0, rows].astype(F32)
        gate = jax.nn.sigmoid(mix_ref[1, rows].astype(F32))
        halves.append(
            jnp.concatenate(
                [(result * gate).astype(BF16), (result * left * gate * (1.0 - gate)).astype(BF16)], axis=1
            )
        )
    grad_mix = jnp.concatenate(halves, axis=0)
    store_rows(gw_ref, slice(0, 2 * piece), dot_tn(normed_ref[...], grad_mix))
    store_rows(gw_ref, slice(2 * piece, 3 * piece), pass_ref[0])
    total[...] += dot_tt(grad_mix[:, :piece], wa_ref[0]) + dot_tt(grad_mix[:, piece:], wb_ref[0])

    @pl.when(step == steps - 1)
    def _():
        unit, scale = norm_parts(x_ref[...])
        grad, gain_row, shift_row = norm_back(total[...], unit, scale, rows_ref[0:1])
        gx_ref[...] = grad_ref[...] + grad
        sums_ref[...] = jnp.zeros_like(sums_ref)
        sums_ref[0:1] = gain_row
        sums_ref[1:2] = shift_row


def conv_back(gconv, next_rim, gated, rim, taps, mixing, normed, conv_blocks, x, grad, rows, passed, frames, depth):
    tokens, width = x.shape
    steps = conv_blocks.shape[0]
    gw_shape = (steps, 2, depth, width // depth // 2, 3 * width // steps)
    gw_spec = spec((1,) + gw_shape[1:], lambda step: (step, 0, 0, 0, 0))
    piece = width // steps
    col = lambda rows_here: spec((rows_here, piece), lambda step: (0, step))
    return call(
        functools.partial(conv_back_kernel, steps, frames),
        steps,
        [
            col(tokens), col(rim.shape[0]), col(tokens), col(rim.shape[0]), col(taps.shape[0]),
            spec((2, tokens, piece), lambda step: (0, 0, step)), full((tokens, width)),
            column(width, piece, 0), column(width, piece, 1),
            full((tokens, width)), full((tokens, width)), full(rows.shape), column(width, piece, 0),
        ],
        [full((tokens, width)), gw_spec, col(taps.shape[0]), full((8, width))],
        [
            struct((tokens, width), F32), struct(gw_shape, BF16),
            struct(taps.shape, F32), struct((8, width), F32),
        ],
        [pltpu.VMEM((RIM + frames, piece), F32), pltpu.VMEM((tokens, width), F32)],
        [gconv, next_rim, gated, rim, taps, mixing, normed, conv_blocks, conv_blocks, x, grad, rows, passed],
        "conv_back",
        4 * tokens * width * width,
    )


def attn_out_back_kernel(steps, grad_ref, att_ref, wo_ref, gatt_ref, gw_ref, sums_ref):
    piece = wo_ref.shape[2]
    branch = grad_ref[...].astype(BF16)
    sums_ref[...] = jnp.broadcast_to(jnp.sum(branch.astype(F32), axis=0, keepdims=True), sums_ref.shape)
    total = dot_tt(branch[:, :piece], wo_ref[0])
    for part in range(1, steps):
        total += dot_tt(branch[:, part * piece : (part + 1) * piece], wo_ref[part])
    gatt_ref[...] = total.astype(BF16)
    for part in range(steps):
        gw_ref[part] = dot_tn(att_ref[...], branch[:, part * piece : (part + 1) * piece]).astype(BF16)


def attn_out_back(grad, attended, attn_blocks):
    tokens, width = grad.shape
    steps = attn_blocks.shape[0]
    piece = width // steps
    return call(
        functools.partial(attn_out_back_kernel, steps),
        1,
        [full((tokens, width)), full((tokens, width)), spec((steps, width, piece), lambda step: (0, 0, 3))],
        [full((tokens, width)), full((steps, width, piece)), full((8, width))],
        [struct((tokens, width), BF16), struct((steps, width, piece), BF16), struct((8, width), F32)],
        [],
        [grad, attended, attn_blocks],
        "attn_out_back",
        2 * tokens * width * width,
    )


def project_back_kernel(steps, counts, gq_ref, *refs):
    gkv_refs, refs = refs[: sum(counts)], refs[sum(counts) :]
    normed_ref, wq_ref, wk_ref, wv_ref, x_ref, grad_ref, rows_ref, pass_ref, *refs = refs
    gx_ref, gw_ref, gbias_ref, sums_ref, total = refs
    step = pl.program_id(0)
    grad_kv = []
    for place in range(2):
        clips, start = [], 0
        for count in counts:
            part = gkv_refs[start][place].astype(F32)
            for ref in gkv_refs[start + 1 : start + count]:
                part += ref[place].astype(F32)
            clips.append(part.astype(BF16))
            start += count
        grad_kv.append(jnp.concatenate(clips))
    piece = wq_ref.shape[2]

    @pl.when(step == 0)
    def _():
        total[...] = jnp.zeros_like(total)

    gbias_ref[...] = jnp.zeros_like(gbias_ref)
    for place, (grad_part, weight) in enumerate(
        [(gq_ref[...], wq_ref), (grad_kv[0], wk_ref), (grad_kv[1], wv_ref)]
    ):
        store_rows(gw_ref, slice(place * piece, (place + 1) * piece), dot_tn(normed_ref[...], grad_part))
        total[...] += dot_tt(grad_part, weight[0])
        gbias_ref[place : place + 1] = jnp.sum(grad_part.astype(F32), axis=0, keepdims=True)
    store_rows(gw_ref, slice(3 * piece, 4 * piece), pass_ref[0])

    @pl.when(step == steps - 1)
    def _():
        unit, scale = norm_parts(x_ref[...])
        grad, gain_row, shift_row = norm_back(total[...], unit, scale, rows_ref[0:1])
        gx_ref[...] = grad_ref[...] + grad
        sums_ref[...] = jnp.zeros_like(sums_ref)
        sums_ref[0:1] = gain_row
        sums_ref[1:2] = shift_row


def project_back(gq, gkv, normed, attn_blocks, x, grad, rows, passed, depth):
    tokens, width = x.shape
    steps = attn_blocks.shape[0]
    gw_shape = (steps, 2, depth, width // depth // 2, 4 * width // steps)
    gw_spec = spec((1,) + gw_shape[1:], lambda step: (step, 0, 0, 0, 0))
    piece = width // steps
    col = spec((tokens, piece), lambda step: (0, step))
    return call(
        functools.partial(project_back_kernel, steps, [len(parts) for parts in gkv]),
        steps,
        [col]
        + [spec((2, tokens // len(gkv), piece), lambda step: (0, 0, step)) for parts in gkv for _ in parts]
        + [full((tokens, width))]
        + [column(width, piece, place) for place in range(3)]
        + [full((tokens, width)), full((tokens, width)), full(rows.shape), column(width, piece, 0)],
        [full((tokens, width)), gw_spec, spec((8, piece), lambda step: (0, step)), full((8, width))],
        [
            struct((tokens, width), F32), struct(gw_shape, BF16),
            struct((8, width), F32), struct((8, width), F32),
        ],
        [pltpu.VMEM((tokens, width), F32)],
        [gq]
        + [part for parts in gkv for part in parts]
        + [normed, attn_blocks, attn_blocks, attn_blocks, x, grad, rows, passed],
        "project_back",
        6 * tokens * width * width,
    )


def stack_rows(*rows):
    return jnp.pad(jnp.stack(rows), ((0, 8 - len(rows)), (0, 0)))


def local(
    inputs, cotangent, ffn1_in, ffn1_out, attn_in, attn_out, conv_in, conv_out, ffn2_in, ffn2_out,
    depthwise, rel_table, norm_gain, shifts, hidden_bias, attn_bias, clip_threshold,
):
    clips, frames, width = inputs.shape
    tokens = clips * frames
    small = jnp.concatenate(
        [depthwise, norm_gain, shifts, attn_bias[:, None], hidden_bias.reshape(depthwise.shape[0], -1)], axis=1
    )
    small = jnp.pad(small, ((0, 0), (0, 128 - small.shape[1])))
    small = lax.all_gather(small, SHARD, axis=0, tiled=True).astype(F32)
    small_rows = jnp.transpose(small[:, :48])
    taps = jnp.pad(small_rows[:KER], ((0, 1), (0, 0)))
    gains = [small_rows[KER + index] for index in range(6)]
    biases = [small_rows[KER + 6 + index] for index in range(10)]
    hidden_rows = jnp.transpose(small[:, 48:56].reshape(-1, 2))
    hidden_biases = [jnp.broadcast_to(hidden_rows[index : index + 1], (8, hidden_rows.shape[1])) for index in range(2)]
    norm_rows = [stack_rows(gains[index], biases[index]) for index in range(6)]
    thirds = [attn_in[:, index * width : (index + 1) * width] for index in range(3)]
    halves = [conv_in[:, :width], conv_in[:, width:]]
    bundles = [(ffn1_in,), (ffn1_out,), (*thirds, attn_out), (*halves, conv_out), (ffn2_in,), (ffn2_out,)]
    piece = width // (lax.axis_size("x") * 2)
    depth = lax.axis_size("z")
    quick = lax.axis_size("x") == 2 and depth == 4
    me = lax.axis_index(SEQ)
    rel_wide = relative_rows(rel_table)
    stream_zero = inputs.reshape(tokens, width)
    rows_one = stack_rows(gains[0], biases[0], biases[6])
    rows_five = stack_rows(gains[4], biases[4], biases[7])
    bias_two = stack_rows(biases[8], biases[9])
    if quick:
        one, two, three, four, five = [Gather(parts, index < 4) for index, parts in enumerate(bundles[:5])]
        six = PlainGather(ffn2_out)
        clock = one.over_z()
        clock = one.first(clock) + two.over_z(clock)
        clock = one.second(clock) + two.first(clock) + three.over_z(clock)
        blocks1 = one.blocks(clock)
        clock = two.second(clock) + three.first(clock) + four.over_z(clock)
        blocks2 = two.blocks(clock)
        five.over_z(clock)
        six.over_z([five.a0])
        clock = three.second(clock) + four.first(clock)
        blocks3 = three.blocks(clock)
        stream_one, normed_one, hidden_one = ffn(stream_zero, rows_one, hidden_biases[0], blocks1, blocks2)
        clock = four.second(clock) + five.first(clock)
        blocks4 = four.blocks(clock)
        normed_two, queries, keys_values = project(stream_one, norm_rows[1], bias_two, blocks3, frames)
        order = jnp.bitwise_xor(me, jnp.arange(4, dtype=jnp.int32))
        where = where_vector(order, me)
        chunks = [[own, swap(own, "core")] for own in keys_values]
        sent0, own5 = slot(clock, keys_values[0], jnp.concatenate([five.b0, five.xb]))
        far0, five.yb = swap(sent0, "x"), swap(own5, "y")
        chunks[0] += [far0, swap(far0, "core")]
        clock = [five.yb, *chunks[0]]
        (sent1,) = slot(clock, keys_values[1])
        far1 = swap(sent1, "x")
        half0 = six.half(0, clock)
        part = attend(queries, 0, clips, chunks[0], where, rel_wide)
        chunks[1] += [far1, swap(far1, "core")]
        clock = [*half0, *part, *chunks[1]]
        (own5,) = slot(clock, jnp.concatenate([five.a0, five.ya]))
        five.xa = swap(own5, "x")
        half1 = six.half(1, clock)
        part = slot(clock, *part)
        attended, tops, log_totals = attend(queries, 1, clips, chunks[1], where, rel_wide, part)
        clock = [five.xa, *half1, attended]
        blocks5 = five.blocks(clock)
        blocks6 = six.blocks(half0 + half1, [blocks5])
    else:
        blocks1, blocks2, blocks3, blocks4, blocks5, blocks6 = [gather_weights(parts) for parts in bundles]
        stream_one, normed_one, hidden_one = ffn(stream_zero, rows_one, hidden_biases[0], blocks1, blocks2)
        normed_two, queries, keys_values = project(stream_one, norm_rows[1], bias_two, blocks3, frames)
        order = jnp.arange(lax.axis_size(SEQ), dtype=jnp.int32)
        where = where_vector(order, me)
        chunks = [list(lax.all_gather(own, SEQ, axis=0)) for own in keys_values]
        part = None
        for clip in range(clips):
            part = attend(queries, clip, clips, chunks[clip], where, rel_wide, part)
        attended, tops, log_totals = part
    stream_two, normed_three, mixing, gated = mix(
        attended, stream_one, stack_rows(gains[2], biases[2], small_rows[47]), blocks3, blocks4
    )
    rim = from_behind(gated.reshape(clips, frames, width)[:, frames - RIM :], SEQ, 1).reshape(-1, width)
    stream_three, convolved = convolve(gated, rim, taps, stream_two, norm_rows[3], blocks4, frames)
    output, grad_four, sums_final, normed_five, hidden_five, _ = ffn(
        stream_three, rows_five, hidden_biases[1], blocks5, blocks6,
        (cotangent.reshape(tokens, width), norm_rows[5]),
    )

    grads_6, grad_three, grads_5, sums_five, bias_five = ffn_back(
        grad_four, stream_three, rows_five, normed_five, hidden_five, blocks5, blocks6, depth, True
    )
    if quick:
        send6, send5 = Scatter(grads_6), Scatter(grads_5)
        send5.over_core(send6.over_core())
    grad_conv, grad_conv_out, sums_conv = norm_silu_back(grad_three, convolved, norm_rows[3], blocks4)
    next_rim = from_behind(grad_conv.reshape(clips, frames, width)[:, :RIM], SEQ, -1).reshape(-1, width)
    clock = []
    if quick:
        clock = send6.first([next_rim])
    grad_two, grads_4, grad_taps, sums_three = conv_back(
        grad_conv, next_rim, gated, rim, taps, mixing, normed_three, blocks4, stream_two, grad_three,
        norm_rows[2], grad_conv_out, frames, depth,
    )
    sides = side_columns(order, me, frames)
    if quick:
        (grad_two,) = slot(clock, grad_two)
        clock = send6.second(clock + [grad_two]) + send5.first(clock + [grad_two])
        send4 = Scatter(grads_4)
        send4.over_core([send5.value])
    grad_attended, grad_attn_out, sums_out = attn_out_back(grad_two, attended, blocks3)
    if quick:
        back, parts = attend_back(
            queries, 0, clips, chunks[0], grad_attended, attended, log_totals, where, rel_wide, sides
        )
        back, *parts = slot(clock, back[0], *parts, back[1], back[2])
        back, parts = (back, *parts[4:]), parts[:4]
        got6 = send6.last()
        beside0, across0 = swap(parts[1], "core"), swap(parts[3], "core")
        sent0 = add(parts[2], across0)
        (sent0,) = slot(clock, sent0)
        clock = [sent0]
        clock = [swap(sent0, "x")] + send5.second(clock) + send4.first(clock)
        kept0 = [parts[0], beside0, clock[0]]
        back, parts = attend_back(
            queries, 1, clips, chunks[1], grad_attended, attended, log_totals, where, rel_wide, sides, back
        )
        grad_q, grad_band, grad_ends = back
        parts = slot(clock, *parts)
        got5 = send5.last()
        beside1, across1 = swap(parts[1], "core"), swap(parts[3], "core")
        sent1 = add(parts[2], across1)
        clock = [sent1]
        clock = [swap(sent1, "x")] + send4.second(clock)
        grad_kv = [kept0, [parts[0], beside1, clock[0]]]
        got4 = send4.last()
    else:
        back, grad_kv = None, []
        for clip in range(clips):
            back, parts = attend_back(
                queries, clip, clips, chunks[clip], grad_attended, attended, log_totals, where, rel_wide, sides, back
            )
            grad_kv.append([lax.psum_scatter(jnp.stack(parts), SEQ, scatter_dimension=0, tiled=True)[0]])
        grad_q, grad_band, grad_ends = back
    grad_one, grads_3, sums_bias, sums_two = project_back(
        grad_q, grad_kv, normed_two, blocks3, stream_one, grad_two, norm_rows[1], grad_attn_out, depth
    )
    if quick:
        send3 = Scatter(grads_3)
        send3.over_core()
    grads_2 = ffn_out_grad(grad_one, hidden_one, blocks1.shape[0], depth)
    if quick:
        send2 = Scatter(grads_2)
        send2.over_core([send3.value])
        (grad_one,) = slot([grads_2], grad_one)
        clock = send3.first(clock + [grads_2])
    _, grad_zero, grads_1, sums_one, bias_one = ffn_back(
        grad_one, stream_zero, rows_one, normed_one, hidden_one, blocks1, blocks2, depth, False
    )
    if quick:
        send1 = Scatter(grads_1)
        send1.over_core([send2.value])
        clock = send3.second(clock + [grads_1]) + send2.first(clock + [grads_1])
        got3 = send3.last()
        clock = send2.second(clock) + send1.first(clock)
        got2 = send2.last()
        clock = send1.second(clock)
        got1 = send1.last()
    else:
        got6, got5, got4, got3, got2, got1 = [
            scatter_grads(value) for value in (grads_6, grads_5, grads_4, grads_3, grads_2, grads_1)
        ]
    rows_in, edge = got5.shape
    early = share_columns([got6.reshape(rows_in, -1), got5, got4])
    later = share_columns([got3])
    final = share_columns([got2.reshape(rows_in, -1), got1])
    fold = got6.size // rows_in
    grad_ffn2_out = unfold(early[:, :, :fold].reshape(-1, *got6.shape), 0, piece)
    grad_ffn2_in = unfold(early, fold, fold + edge)
    starts = [fold + edge + index * piece for index in range(3)]
    grad_a, grad_b, grad_conv_out = [unfold(early, start, start + piece) for start in starts]
    grad_q, grad_k, grad_v, grad_attn_out = [unfold(later, index * piece, (index + 1) * piece) for index in range(4)]
    grad_ffn1_out = unfold(final[:, :, :fold].reshape(-1, *got2.shape), 0, piece)
    grad_ffn1_in = unfold(final, fold, fold + edge)
    small_sums = [
        grad_taps[:KER],
        jnp.stack([sums_one[0], sums_two[0], sums_three[0], sums_conv[0], sums_five[0], sums_final[0]]),
        jnp.stack([sums_one[1], sums_two[1], sums_three[1], sums_conv[1], sums_five[1], sums_final[1]]),
        jnp.stack([sums_one[2], sums_five[2], sums_bias[0], sums_bias[2], sums_out[0]]),
        bias_one[0].reshape(-1, width),
        bias_five[0].reshape(-1, width),
        jnp.pad(table_grad(grad_band, grad_ends).reshape(-1), (0, 5 * width - REL * HD)).reshape(5, width),
    ]
    peaks = jnp.broadcast_to(jnp.pad(jnp.max(tops, axis=0), (0, width - 128)), (8, width))
    small_sum, peaks = combine_all(jnp.concatenate(small_sums), peaks)
    head_max = peaks[0, :H]
    qk_scale = jnp.sqrt(clip_threshold / jnp.maximum(head_max, clip_threshold))
    grad_rel_table = small_sum[-5:].reshape(-1)[: REL * HD].reshape(REL, HD)
    share = depthwise.shape[0]
    own = lax.dynamic_slice_in_dim(small_sum[:48], lax.axis_index(SHARD) * share, share, axis=1)
    own = jnp.transpose(own)
    hidden_sums = small_sum[48:56].reshape(2, -1)
    share = hidden_bias.shape[0]
    hidden_sums = lax.dynamic_slice_in_dim(hidden_sums, lax.axis_index(SHARD) * share, share, axis=1)
    return (
        output.reshape(inputs.shape),
        grad_zero.reshape(inputs.shape),
        grad_ffn1_in,
        grad_ffn1_out,
        jnp.concatenate([grad_q, grad_k, grad_v], axis=1),
        grad_attn_out,
        jnp.concatenate([grad_a, grad_b], axis=1),
        grad_conv_out,
        grad_ffn2_in,
        grad_ffn2_out,
        own[:, :KER],
        grad_rel_table,
        own[:, KER : KER + 6],
        own[:, KER + 6 : KER + 16],
        jnp.transpose(hidden_sums),
        own[:, KER + 16],
        head_max,
        qk_scale,
    )


def solution(mesh):
    rows = P(SHARD, None)
    tokens = P(SHARD, SEQ, None)
    return jax.shard_map(
        local,
        mesh=refine(mesh),
        in_specs=(tokens, tokens) + (rows,) * 9 + (P(),) + (rows,) * 3 + (P(SHARD), P()),
        out_specs=(tokens, tokens) + (rows,) * 9 + (P(),) + (rows,) * 3 + (P(SHARD), P(), P()),
        check_vma=False,
    )
```
